512 devices in a mesh: pair: 32 (over z_lo, y), row: 4 (over z_hi, core), col: 4 (over x).
Axes of the slice: x: 4, y: 4, z: 16 (z_hi: 2, z_lo: 8; z = z_hi * 8 + z_lo), core: 2. Of those that a mesh axis runs over, the one named last changes fastest.
Arguments:
- intersection: float32 [32, 1280, 1280], P('pair', 'row', 'col'), as said below
- children: float32 [32, 1280, 1280], P('pair', 'row', 'col'), as said below
- band_start: int32 [10], replicated, may hold values from 0 to 2, as said below
- assignment: int32 [32, 5], replicated, may hold values from 0 to 1, as said below
Outputs:
- refined: float32 [32, 1280, 1280], P('pair', 'row', 'col')
- deviation: float32 [32, 1280, 1280], P('pair', 'row', 'col')
The draws below stay inside these ranges and needn't reach their ends.
Inputs may be any that keep to these rules, and one draw needn't show every extreme that they name: band_start[i] <= i < band_start[i] + 8 for every block row i; the first block row starts at 0 and the last at 2. Every merge's row of assignment holds both values. `intersection`: each merge's matrix is symmetric with a positive diagonal that outweighs its off-diagonal part. `children`: each matrix is symmetric and is zero outside its upper left and lower right quadrants of order 1280 / 2.
All inputs are finite; a program needn't handle non-finite values.
Results may differ from the reference program's by a relative error of at most 0.0003.
Values sent between devices are 32-bit elements; how exact they have to be, the bound alone decides.
A program may use at most 64 MiB of HBM per device.

```python
import jax
import jax.numpy as jnp
from jax import lax

BLK = 128
BAND = 8
M = 1280
MB = 10
MERGES = 32


def draw_intersection(key, part):
    key = jax.random.fold_in(key, 11)
    first, second = jax.random.split(key)
    noise = 0.35 * jax.random.normal(first, (MERGES, M, M), jnp.float32) / jnp.sqrt(jnp.float32(M))
    diagonal = jax.random.uniform(second, (MERGES, M), jnp.float32, 2.0, 6.0)
    symmetric = 0.5 * (noise + jnp.swapaxes(noise, 1, 2))
    eye = jnp.eye(M, dtype=jnp.float32)
    return symmetric * (1.0 - eye) + eye * diagonal[:, :, None]


def draw_children(key, part):
    key = jax.random.fold_in(key, 12)
    first, second = jax.random.split(key)
    half = M // 2
    noise = 0.08 * jax.random.normal(first, (MERGES, M, M), jnp.float32) / jnp.sqrt(jnp.float32(half))
    diagonal = jax.random.uniform(second, (MERGES, M), jnp.float32, 0.3, 0.7)
    symmetric = 0.5 * (noise + jnp.swapaxes(noise, 1, 2))
    eye = jnp.eye(M, dtype=jnp.float32)
    full = symmetric * (1.0 - eye) + eye * diagonal[:, :, None]
    index = jnp.arange(M)
    same = (index[:, None] < half) == (index[None, :] < half)
    return jnp.where(same[None], full, jnp.float32(0.0))


def draw_band_start(key, part):
    key = jax.random.fold_in(key, 13)
    index = jnp.arange(MB, dtype=jnp.int32)
    back = jax.random.randint(key, (MB,), 0, BAND, dtype=jnp.int32)
    return jnp.clip(index - back, 0, MB - BAND).astype(jnp.int32)


def draw_assignment(key, part):
    key = jax.random.fold_in(key, 14)
    first, second = jax.random.split(key)
    width = MB // 2
    values = jax.random.randint(first, (MERGES, width), 0, 2, dtype=jnp.int32)
    place = jax.random.randint(second, (MERGES,), 0, width, dtype=jnp.int32)
    columns = jnp.arange(width, dtype=jnp.int32)
    values = jnp.where(columns[None, :] == place[:, None], 0, values)
    values = jnp.where(columns[None, :] == ((place + 1) % width)[:, None], 1, values)
    return values.astype(jnp.int32)


def setup_inputs(seed: int = 0) -> dict:
    streams_of = jax.random.split(jax.random.key(seed), 5)
    intersection = draw_intersection(jax.random.fold_in(streams_of[4], 71), 0)
    children = draw_children(jax.random.fold_in(streams_of[4], 71), 0)
    band_start = draw_band_start(jax.random.fold_in(streams_of[4], 71), 0)
    assignment = draw_assignment(jax.random.fold_in(streams_of[4], 71), 0)
    return dict(intersection=intersection, children=children, band_start=band_start, assignment=assignment)


def band_mask(band_start):
    index = jnp.arange(M, dtype=jnp.int32) // BLK
    start = band_start[index]
    first = (index[None, :] >= start[:, None]) & (index[None, :] < start[:, None] + BAND)
    second = (index[:, None] >= start[None, :]) & (index[:, None] < start[None, :] + BAND)
    return first | second


def refine_one(pieces):
    banded, factor = pieces
    hp = lax.Precision.HIGHEST
    image = jnp.dot(banded, factor, precision=hp, preferred_element_type=jnp.float32)
    congruence = jnp.dot(factor, image, precision=hp, preferred_element_type=jnp.float32)
    correction = jnp.dot(factor, congruence, precision=hp, preferred_element_type=jnp.float32)
    identity = jnp.eye(M, dtype=jnp.float32)
    return 1.5 * factor - 0.5 * correction, identity - congruence


def reference(intersection, children, band_start, assignment):
    keep = band_mask(band_start)
    half = M // 2
    from_left = jnp.roll(children, 1, axis=0)
    from_right = jnp.roll(children, -1, axis=0)
    quarter_rows = jnp.arange(half, dtype=jnp.int32) // BLK
    selector = assignment[:, quarter_rows]
    chosen = jnp.where(selector[:, :, None] == 0, from_left[:, half:, half:], from_right[:, half:, half:])
    factor = children.at[:, half:, half:].set(chosen)

    def one(index):
        banded = jnp.where(keep, intersection[index], jnp.float32(0.0))
        return refine_one((banded, factor[index]))

    refined, deviation = lax.map(one, jnp.arange(MERGES, dtype=jnp.int32))
    return refined, deviation
```

```python
import jax
import jax.numpy as jnp
from jax import lax
from jax.experimental import pallas as pl
from jax.experimental.pallas import tpu as pltpu
from jax.sharding import PartitionSpec as P

BLK = 128
BAND = 8
TILE = 320
HALF = 640
DIAG = 576
OFFD = 800
PART = 400
MESH = pl.DeviceIdType.MESH
F32 = jnp.float32
BF16 = jnp.bfloat16


def place():
    p = lax.axis_index("pair")
    row = lax.axis_index("row")
    x = lax.axis_index("col")
    h, c = row // 2, row % 2
    return p, h, c, x, (x + 2 * h) % 4


def device(p, h, c, u):
    return ((p + 32) % 32, 2 * h + c, (u + 2 * h) % 4)


def gather_kernel(assign, s, k, sq, lt, gd, go, raw, pkd, pko, zin, zout, send, recv):
    p, h, c, x, u = place()
    home = u < 2
    guest = u >= 2
    plane0 = h == 0
    plane1 = h == 1
    diag_home = home & (u == c)
    diag_guest = guest & (u - 2 == c)
    off_home = (u == 0) & (c == 1)
    relay = guest & (c == 1)
    landing = home & (c == 1)
    other = device(p, h, 1 - c, u)

    def copy(i, src, dst, to):
        return pltpu.make_async_remote_copy(
            src_ref=src, dst_ref=dst, send_sem=send.at[i], recv_sem=recv.at[i],
            device_id=to, device_id_type=MESH,
        )

    def on(cond, *acts):
        @pl.when(cond)
        def _():
            for act in acts:
                act()

    barrier = pltpu.get_barrier_semaphore()
    near = [device(p, h, c, (u + 1) % 4), device(p, h, c, (u + 2) % 4), device(p, h, c, (u + 3) % 4), other]
    far = [device(p, 1 - h, c, (u + 2) % 4)]
    for q in (p - 1, p + 1):
        far += [device(q, h, c, v) for v in range(4)]
    for d in far + near:
        pl.semaphore_signal(barrier, inc=1, device_id=d, device_id_type=MESH)

    own_s = 2 * c + u % 2
    far_s = 2 * c + 1 - u % 2
    first = jnp.where(home, 2 * c + u, 2 * c + 3 - u)
    second = jnp.where(home, 2 * c + 1 - u, 2 * c + u - 2)

    @pl.when(diag_home)
    def _():
        pkd[0:320] = k[:, 0:128]
        pkd[320:512] = k[128:320, 128:256]
        pkd[512:576, 0:64] = k[256:320, 256:320]
        pkd[512:576, 64:128] = jnp.zeros((64, 64), F32)

    @pl.when(off_home)
    def _():
        pko[0:320] = k[:, 0:128]
        pko[320:640] = k[:, 128:256]
        pko[640:800] = jnp.concatenate([k[0:160, 256:320], k[160:320, 256:320]], axis=1)

    sq[own_s] = s[...]

    @pl.when(home & plane0)
    def _():
        lt[first] = k[...]

    sx = copy(0, s, sq.at[own_s], device(p, h, c, u + 1 - 2 * (u % 2)))
    sc0 = copy(1, s, sq.at[own_s], other)
    sc1 = copy(2, sq.at[far_s], sq.at[far_s], other)
    yr = copy(3, k, raw.at[0], device(p + 1, h, c, u))
    yl = copy(4, k, raw.at[1], device(p - 1, h, c, u))
    hh = copy(5, lt.at[first], lt.at[first], device(p, h, c, 1 - u))
    hg = copy(6, lt.at[first], lt.at[first], device(p, h, c, 3 - u))
    gg = copy(7, lt.at[first], lt.at[first], device(p, h, c, 5 - u))
    ca = copy(8, lt.at[first], lt.at[first], other)
    cb = copy(9, lt.at[second], lt.at[second], other)
    zslot = jnp.where(plane0, 0, 2)
    zd = copy(10, pkd, gd.at[zslot], device(p, 1 - h, c, (u + 2) % 4))
    fr = copy(11, gd.at[2], gd.at[0], device(p + 1, h, c, u))
    fl = copy(12, gd.at[2], gd.at[1], device(p - 1, h, c, u))
    gs0 = copy(13, gd.at[0], gd.at[0], other)
    gs1 = copy(14, gd.at[1], gd.at[1], other)
    r0 = copy(15, pko.at[pl.ds(0, PART)], zin, device(p, h, c, 3))
    r1 = copy(16, pko.at[pl.ds(PART, PART)], zin, device(p, h, c, 2))
    zo = copy(17, zin, zout, device(p, 1 - h, c, (u + 2) % 4))
    part = 1 - u % 2
    begin = pl.multiple_of(part * PART, 8)
    ahead = jnp.where(plane0, p + 1, p)
    spread = [
        [copy(18 + part, zout, go.at[0, pl.ds(begin, PART)], device(ahead, h, c, 2)),
         copy(20 + part, zout, go.at[0, pl.ds(begin, PART)], device(ahead, h, c, 3))],
        [copy(22 + part, zout, go.at[1, pl.ds(begin, PART)], device(p - 1, h, c, 2)),
         copy(24 + part, zout, go.at[1, pl.ds(begin, PART)], device(p - 1, h, c, 3))],
    ]
    arrived = [
        [copy(18 + 2 * (u - 2) + i, zout, go.at[0, pl.ds(i * PART, PART)], other) for i in range(2)],
        [copy(22 + 2 * (u - 2) + i, zout, go.at[1, pl.ds(i * PART, PART)], other) for i in range(2)],
    ]
    os0 = copy(26, go.at[0], go.at[0], other)
    os1 = copy(27, go.at[1], go.at[1], other)

    pl.semaphore_wait(barrier, len(near) + len(far))

    on(off_home, r0.start, r1.start)
    on(diag_home, zd.start)
    on(home & plane1, yr.start, yl.start)
    on(home & plane0, hg.start, hh.start, ca.start)
    sx.start()
    sc0.start()

    on(relay & (u == 3), r0.wait_recv)
    on(relay & (u == 2), r1.wait_recv)
    on(relay, zo.start)

    @pl.when(home & plane1)
    def _():
        yr.wait_recv()
        yl.wait_recv()
        for j in range(5):
            rows = pl.ds(64 * j, 64)
            lt[first, rows] = jnp.where(assign[p, (5 * c + j) // 2] == 0, raw[0, rows], raw[1, rows])
        hg.start()
        hh.start()
        ca.start()

    sx.wait_recv()
    sc1.start()

    on(guest & plane0, hg.wait_recv, gg.start, ca.start, gg.wait_recv, cb.start)
    on(home & plane0, hh.wait_recv, cb.start)

    on(diag_guest & plane0, zd.wait_recv, fr.start, fl.start)
    on(landing, zo.wait_recv, spread[0][0].start, spread[0][1].start)
    on(landing & plane0, spread[1][0].start, spread[1][1].start)

    on(guest & plane1, hg.wait_recv, gg.start, ca.start, gg.wait_recv, cb.start)
    on(home & plane1, hh.wait_recv, cb.start)

    on(diag_guest & plane1, zd.wait_recv, gs0.start)
    on(diag_guest & plane0, fr.wait_recv, gs0.start, fl.wait_recv, gs1.start)
    on(relay, arrived[0][0].wait_recv, arrived[0][1].wait_recv, os0.start)
    on(relay & plane0, arrived[1][0].wait_recv, arrived[1][1].wait_recv, os1.start)

    sc0.wait_recv()
    sc1.wait_recv()
    ca.wait_recv()
    cb.wait_recv()
    on(guest & (u - 2 != c), gs0.wait_recv)
    on(guest & (u - 2 != c) & plane0, gs1.wait_recv)
    on(guest & (c == 0), os0.wait_recv)
    on(guest & (c == 0) & plane0, os1.wait_recv)

    sx.wait_send()
    sc0.wait_send()
    sc1.wait_send()
    ca.wait_send()
    cb.wait_send()
    on(home, hh.wait_send, hg.wait_send)
    on(guest, gg.wait_send)
    on(home & plane1, yr.wait_send, yl.wait_send)
    on(diag_home, zd.wait_send)
    on(off_home, r0.wait_send, r1.wait_send)
    on(relay, zo.wait_send, os0.wait_send)
    on(relay & plane0, os1.wait_send)
    on(diag_guest, gs0.wait_send)
    on(diag_guest & plane0, fr.wait_send, fl.wait_send, gs1.wait_send)
    on(landing, spread[0][0].wait_send, spread[0][1].wait_send)
    on(landing & plane0, spread[1][0].wait_send, spread[1][1].wait_send)


def split(v):
    hi = v.astype(BF16)
    return hi, (v - hi.astype(F32)).astype(BF16)


def dot3(ah, al, bh, bl):
    d = lambda a, b: jnp.dot(a, b, preferred_element_type=F32)
    return d(ah, bh) + (d(ah, bl) + d(al, bh))


def square(v):
    a, b, e = v[0:320], v[320:512], v[512:576, 0:64]
    r0 = jnp.concatenate([a[0:128], a[128:320].T], axis=1)
    r1 = jnp.concatenate([a[128:256], b[0:128], b[128:192].T], axis=1)
    r2 = jnp.concatenate([a[256:320], b[128:192], e], axis=1)
    return jnp.concatenate([r0, r1, r2], axis=0)


def oblong(v):
    e = v[640:800]
    return jnp.concatenate([v[0:320], v[320:640], jnp.concatenate([e[:, 0:64], e[:, 64:128]], axis=0)], axis=1)


def multiply_kernel(band, assign, k, sq, lt, gd, go, refined, deviation, lh, ll, sh, sl, th, tl, gh, gl, ch, cl):
    p, h, c, x, u = place()
    home = u < 2
    for r in range(2):
        rows = pl.ds(TILE * r, TILE)
        lh[rows], ll[rows] = split(jnp.concatenate([lt[2 * r], lt[2 * r + 1]], axis=1))
    hc = x // 2
    cols = lax.broadcasted_iota(jnp.int32, (1, HALF), 1) // BLK
    starts = jnp.zeros((1, HALF), jnp.int32)
    for j in range(5):
        starts = jnp.where(cols == j, band[5 * hc + j], starts)
    cols = cols + 5 * hc
    for i in range(10):
        r, local = i // 5, pl.ds(64 * (i % 5), 64)
        v = jnp.concatenate([sq[2 * r, local], sq[2 * r + 1, local]], axis=1)
        bi = 5 * h + i // 2
        st = band[bi]
        keep = ((cols >= st) & (cols < st + BAND)) | ((bi >= starts) & (bi < starts + BAND))
        rows = pl.ds(64 * i, 64)
        sh[rows], sl[rows] = split(jnp.where(keep, v, 0.0))

    @pl.loop(0, 5)
    def _(i):
        rows = pl.ds(pl.multiple_of(i * 128, 128), 128)
        th[rows], tl[rows] = split(dot3(lh[rows], ll[rows], sh[...], sl[...]))

    @pl.when(home)
    def _():
        for r in range(2):
            rows = pl.ds(TILE * r, TILE)
            gh[rows], gl[rows] = split(lt[2 * r + u])

    def put(r, v):
        rows = pl.ds(TILE * r, TILE)
        gh[rows], gl[rows] = split(v)

    def chosen(r, unpack, ref):
        a, b = unpack(ref[0]), unpack(ref[1])
        out = []
        for j in range(5):
            sel = assign[p, (5 * r + j) // 2] == 0
            out.append(jnp.where(sel, a[64 * j:64 * j + 64], b[64 * j:64 * j + 64]))
        return jnp.concatenate(out, axis=0)

    flipped = lambda v: oblong(v).T

    @pl.when((u == 2) & (h == 1))
    def _():
        put(0, square(gd[0]))
        put(1, oblong(go[0]))

    @pl.when((u == 3) & (h == 1))
    def _():
        put(0, flipped(go[0]))
        put(1, square(gd[0]))

    @pl.when((u == 2) & (h == 0))
    def _():
        put(0, chosen(0, square, gd))
        put(1, chosen(1, oblong, go))

    @pl.when((u == 3) & (h == 0))
    def _():
        put(0, chosen(0, flipped, go))
        put(1, chosen(1, square, gd))

    for r in range(2):
        rows = pl.ds(TILE * r, TILE)
        v = dot3(th[rows], tl[rows], gh[...], gl[...])
        ch[rows], cl[rows] = split(v)

        @pl.when(c == r)
        def _():
            eye = lax.broadcasted_iota(jnp.int32, (TILE, TILE), 0) == lax.broadcasted_iota(jnp.int32, (TILE, TILE), 1)
            deviation[...] = jnp.where(eye & (2 * h + c == x), 1.0, 0.0) - v

    rows = pl.ds(pl.multiple_of(TILE * c, TILE), TILE)
    corr = dot3(lh[rows], ll[rows], ch[...], cl[...])

    @pl.when(home)
    def _():
        refined[...] = 1.5 * lt[2 * c + u] - 0.5 * corr

    @pl.when(u >= 2)
    def _():
        refined[...] = 1.5 * k[...] - 0.5 * corr


def on_device(intersection, children, band_start, assignment):
    s, k = intersection[0], children[0]
    vm = pl.BlockSpec(memory_space=pltpu.VMEM)
    sm = pl.BlockSpec(memory_space=pltpu.SMEM)
    shape = lambda *d: jax.ShapeDtypeStruct(d, F32)
    sq, lt, gd, go = pl.pallas_call(
        gather_kernel,
        out_shape=(shape(4, TILE, TILE), shape(4, TILE, TILE), shape(3, DIAG, BLK), shape(2, OFFD, BLK)),
        in_specs=[sm, vm, vm],
        out_specs=(vm, vm, vm, vm),
        scratch_shapes=[
            pltpu.VMEM((2, TILE, TILE), F32),
            pltpu.VMEM((DIAG, BLK), F32),
            pltpu.VMEM((OFFD, BLK), F32),
            pltpu.VMEM((PART, BLK), F32),
            pltpu.VMEM((PART, BLK), F32),
            pltpu.SemaphoreType.DMA((28,)),
            pltpu.SemaphoreType.DMA((28,)),
        ],
        compiler_params=pltpu.CompilerParams(
            collective_id=0, has_side_effects=True, vmem_limit_bytes=32 << 20
        ),
        name="gather",
    )(assignment, s, k)
    half = lambda n: pltpu.VMEM((HALF, n), BF16)
    refined, deviation = pl.pallas_call(
        multiply_kernel,
        out_shape=(shape(TILE, TILE), shape(TILE, TILE)),
        in_specs=[sm, sm, vm, vm, vm, vm, vm],
        out_specs=(vm, vm),
        scratch_shapes=[half(HALF)] * 6 + [half(TILE)] * 4,
        compiler_params=pltpu.CompilerParams(vmem_limit_bytes=40 << 20),
        name="multiply",
    )(band_start, assignment, k, sq, lt, gd, go)
    return refined[None], deviation[None]


def solution(mesh):
    spec = P("pair", "row", "col")
    return jax.shard_map(
        on_device, mesh=mesh, in_specs=(spec, spec, P(), P()), out_specs=(spec, spec), check_vma=False
    )
```

```python
import jax
import jax.numpy as jnp
from jax import lax
from jax.experimental import pallas as pl
from jax.experimental.pallas import tpu as pltpu
from jax.sharding import PartitionSpec as P

BLK = 128
BAND = 8
TILE = 320
HALF = 640
DIAG = 576
OFFD = 800
PART = 400
MESH = pl.DeviceIdType.MESH
F32 = jnp.float32
BF16 = jnp.bfloat16


def place():
    p = lax.axis_index("pair")
    row = lax.axis_index("row")
    x = lax.axis_index("col")
    h, c = row // 2, row % 2
    return p, h, c, x, (x + 2 * h) % 4


def device(p, h, c, u):
    return ((p + 32) % 32, 2 * h + c, (u + 2 * h) % 4)


def split(v):
    hi = v.astype(BF16)
    return hi, (v - hi.astype(F32)).astype(BF16)


def dot3(ah, al, bh, bl):
    d = lambda a, b: jnp.dot(a, b, preferred_element_type=F32)
    return d(ah, bh) + (d(ah, bl) + d(al, bh))


def square(v):
    a, b, e = v[0:320], v[320:512], v[512:576, 0:64]
    r0 = jnp.concatenate([a[0:128], a[128:320].T], axis=1)
    r1 = jnp.concatenate([a[128:256], b[0:128], b[128:192].T], axis=1)
    r2 = jnp.concatenate([a[256:320], b[128:192], e], axis=1)
    return jnp.concatenate([r0, r1, r2], axis=0)


def oblong(v):
    e = v[640:800]
    return jnp.concatenate([v[0:320], v[320:640], jnp.concatenate([e[:, 0:64], e[:, 64:128]], axis=0)], axis=1)


def flipped(v):
    return oblong(v).T


def gather_kernel(assign, s_hbm, k_hbm, sp, lp, gd, go, s, k, pko, zb, local, send, recv):
    p, h, c, x, u = place()
    home = u < 2
    guest = u >= 2
    plane0 = h == 0
    plane1 = h == 1
    high = x >= 2
    diag_home = home & (u == c)
    off_home = (u == 0) & (c == 1)
    relay = guest & (c == 1)
    landing = home & (c == 1)
    holds_diag = c == x % 2
    other = device(p, h, 1 - c, u)
    used = [0]

    def copy(src, dst, to, which=0, ways=1):
        i = used[0] + which
        used[0] += ways
        return pltpu.make_async_remote_copy(
            src_ref=src, dst_ref=dst, send_sem=send.at[i], recv_sem=recv.at[i],
            device_id=to, device_id_type=MESH,
        )

    def on(cond, *acts):
        @pl.when(cond)
        def _():
            for act in acts:
                act()

    def cut(ref, n, parts):
        return [ref.at[pl.ds(i * (n // parts), n // parts)] for i in range(parts)]

    def copies(src, dst, n, parts, to):
        return [copy(a, b, to) for a, b in zip(cut(src, n, parts), cut(dst, n, parts))]

    load_k = pltpu.make_async_copy(k_hbm, k, local.at[0])
    load_s = pltpu.make_async_copy(s_hbm, s, local.at[1])
    load_k.start()
    load_s.start()
    barrier = pltpu.get_barrier_semaphore()
    near = [device(p, h, c, (u + 1) % 4), device(p, h, c, (u + 2) % 4), device(p, h, c, (u + 3) % 4), other]
    near += [device(p, h, 1 - c, (u + 1) % 4), device(p, h, 1 - c, (u + 2) % 4), device(p, h, 1 - c, (u + 3) % 4)]
    far = [device(p, 1 - h, c, (u + 2) % 4)]
    for q in (p - 1, p + 1):
        far += [device(q, h, c, v) for v in range(4)]
        far += [device(q, h, 1 - c, v) for v in range(4)]
    for d in far + near:
        pl.semaphore_signal(barrier, inc=1, device_id=d, device_id_type=MESH)

    own_s = 2 * c + u % 2
    far_s = 2 * c + 1 - u % 2
    first = jnp.where(home, 2 * c + u, 2 * c + 3 - u)
    second = jnp.where(home, 2 * c + 1 - u, 2 * c + u - 2)

    def pack(ref, v):
        ref[0:320] = v[:, 0:128]
        ref[320:640] = v[:, 128:256]
        ref[640:800] = jnp.concatenate([v[0:160, 256:320], v[160:320, 256:320]], axis=1)

    load_k.wait()

    @pl.when(diag_home)
    def _():
        gd[2, 0:320] = k[:, 0:128]
        gd[2, 320:512] = k[128:320, 128:256]
        gd[2, 512:576, 0:64] = k[256:320, 256:320]
        gd[2, 512:576, 64:128] = jnp.zeros((64, 64), F32)

    @pl.when(off_home)
    def _():
        pack(pko, k)

    @pl.when(home & plane0)
    def _():
        pack(lp.at[first], k)

    load_s.wait()
    pack(sp.at[own_s], s)

    twin = device(p, 1 - h, c, (u + 2) % 4)
    r0 = copies(pko.at[pl.ds(0, PART)], zb, PART, 2, device(p, h, c, 3))
    r1 = copies(pko.at[pl.ds(PART, PART)], zb, PART, 2, device(p, h, c, 2))
    zo = copies(zb, zb, PART, 2, twin)
    zslot = jnp.where(plane0, 0, 2)
    zd = copies(gd.at[2], gd.at[zslot], DIAG, 2, twin)
    fr = copies(gd.at[2], gd.at[0], DIAG, 2, device(p + 1, h, c, u))
    fl = copies(gd.at[2], gd.at[1], DIAG, 2, device(p - 1, h, c, u))
    gs0 = copies(gd.at[0], gd.at[0], DIAG, 2, other)
    gs1 = copies(gd.at[1], gd.at[1], DIAG, 2, other)
    part = 1 - x % 2
    begin = pl.multiple_of(part * PART, 8)
    base = jnp.where(high, 0, 2)
    ahead = jnp.where(high, p, p + 1)
    spread0 = [[], []]
    spread1 = [[], []]
    arrived0 = []
    arrived1 = []
    for i in range(2):
        for slot, q, out, came in ((0, ahead, spread0, arrived0), (1, p - 1, spread1, arrived1)):
            target = (q + 32) % 32, 2 * h + 1 - i, base + i
            for j in range(2):
                at = used[0]
                dst = go.at[slot, pl.ds(begin + j * (PART // 2), PART // 2)]
                out[j].append(copy(zb.at[pl.ds(j * (PART // 2), PART // 2)], dst, target, part, 2))
                if i == 0:
                    came.append((at, j))
    used_go = used[0]
    span = 8

    def landed(at, j, n, slot):
        i = at + n + (x % 2) * span
        dst = go.at[slot, pl.ds(n * PART + j * (PART // 2), PART // 2)]
        return pltpu.make_async_remote_copy(
            src_ref=zb.at[pl.ds(0, PART // 2)], dst_ref=dst, send_sem=send.at[i], recv_sem=recv.at[i],
            device_id=other, device_id_type=MESH,
        )

    came0 = [landed(at, j, n, 0) for at, j in arrived0 for n in range(2)]
    came1 = [landed(at, j, n, 1) for at, j in arrived1 for n in range(2)]
    os0 = copy(go.at[0], go.at[0], other)
    os1 = copy(go.at[1], go.at[1], other)
    sx = copy(sp.at[own_s], sp.at[own_s], device(p, h, c, u + 1 - 2 * (u % 2)))
    sc0 = copy(sp.at[own_s], sp.at[own_s], other)
    sc1 = copy(sp.at[far_s], sp.at[far_s], other)
    hh = copy(lp.at[first], lp.at[first], device(p, h, c, 1 - u))
    hg = copies(lp.at[first], lp.at[first], OFFD, 2, device(p, h, c, 3 - u))
    gg = copies(lp.at[first], lp.at[first], OFFD, 2, device(p, h, c, 5 - u))
    ca = copy(lp.at[first], lp.at[first], other)
    cb = copy(lp.at[second], lp.at[second], other)

    starts = lambda cs: [d.start for d in cs]
    arrives = lambda cs: [d.wait_recv for d in cs]
    leaves = lambda cs: [d.wait_send for d in cs]

    pl.semaphore_wait(barrier, len(near) + len(far))

    on(off_home, r0[0].start, r1[0].start, r0[1].start, r1[1].start)
    on(diag_home, *starts(zd))
    on(diag_home & plane1, fr[0].start, fl[0].start, fr[1].start, fl[1].start)
    on(home & plane0, *starts(hg), hh.start, ca.start)
    sx.start()
    sc0.start()

    for j in range(2):
        on(relay & (u == 3), r0[j].wait_recv)
        on(relay & (u == 2), r1[j].wait_recv)
        on(relay, zo[j].start)
        on(relay & plane1, *starts(spread0[j]), *starts(spread1[j]))

    def settle(unpack, ref):
        a, b = unpack(ref[0]), unpack(ref[1])
        out = []
        for j in range(5):
            sel = assign[p, (5 * c + j) // 2] == 0
            out.append(jnp.where(sel, a[64 * j:64 * j + 64], b[64 * j:64 * j + 64]))
        pack(lp.at[first], jnp.concatenate(out, axis=0))

    def begin_left():
        for d in hg:
            d.start()
        hh.start()
        ca.start()

    @pl.when(diag_home & plane1)
    def _():
        for d in fr + fl:
            d.wait_recv()
        settle(square, gd)
        begin_left()

    @pl.when(home & (u != c) & plane1)
    def _():
        for d in came0 + came1:
            d.wait_recv()

        @pl.when(u == 0)
        def _():
            settle(oblong, go)

        @pl.when(u == 1)
        def _():
            settle(flipped, go)

        begin_left()

    sx.wait_recv()
    sc1.start()

    def left_side():
        for d, e in zip(hg, gg):
            d.wait_recv()
            e.start()
        ca.start()
        for d in gg:
            d.wait_recv()
        cb.start()

    on(guest & plane0, left_side)
    on(home & plane0, hh.wait_recv, cb.start)

    for j in range(2):
        on(guest & plane0 & holds_diag, zd[j].wait_recv, fr[j].start, fl[j].start)
        on(landing, zo[j].wait_recv, *starts(spread0[j]))
        on(landing & plane0, *starts(spread1[j]))

    on(guest & plane1, left_side)
    on(home & plane1, hh.wait_recv, cb.start)

    for j in range(2):
        on(guest & plane1 & holds_diag, zd[j].wait_recv, gs0[j].start)
        on(guest & plane0 & holds_diag, fr[j].wait_recv, gs0[j].start, fl[j].wait_recv, gs1[j].start)
    on(guest & ~holds_diag, *arrives(came0), os0.start)
    on(guest & plane0 & ~holds_diag, *arrives(came1), os1.start)

    sc0.wait_recv()
    sc1.wait_recv()
    ca.wait_recv()
    cb.wait_recv()
    on(guest & ~holds_diag, *arrives(gs0))
    on(guest & ~holds_diag & plane0, *arrives(gs1))
    on(guest & holds_diag, os0.wait_recv)
    on(guest & holds_diag & plane0, os1.wait_recv)

    for d in (sx, sc0, sc1, ca, cb):
        d.wait_send()
    on(home, hh.wait_send, *leaves(hg))
    on(guest, *leaves(gg))
    on(diag_home, *leaves(zd))
    on(high & holds_diag, *leaves(fr + fl))
    on(off_home, *leaves(r0 + r1))
    on(relay, *leaves(zo))
    on(guest & ~holds_diag, os0.wait_send)
    on(guest & ~holds_diag & plane0, os1.wait_send)
    on(guest & holds_diag, *leaves(gs0))
    on(guest & holds_diag & plane0, *leaves(gs1))
    on((c == 1) & (~high | plane1), *leaves(spread0[0] + spread0[1]))
    on((c == 1) & ~high, *leaves(spread1[0] + spread1[1]))


def multiply_kernel(band, assign, k, sp, lp, gd, go, refined, deviation, lh, ll, sh, sl, th, tl, gh, gl, ch, cl):
    p, h, c, x, u = place()
    home = u < 2
    for r in range(2):
        rows = pl.ds(TILE * r, TILE)
        lh[rows], ll[rows] = split(jnp.concatenate([oblong(lp[2 * r]), oblong(lp[2 * r + 1])], axis=1))
    hc = x // 2
    cols = lax.broadcasted_iota(jnp.int32, (1, HALF), 1) // BLK
    starts = jnp.zeros((1, HALF), jnp.int32)
    for j in range(5):
        starts = jnp.where(cols == j, band[5 * hc + j], starts)
    cols = cols + 5 * hc
    for i in range(10):
        r, local = i // 5, 64 * (i % 5)
        if i % 5 == 0:
            whole = jnp.concatenate([oblong(sp[2 * r]), oblong(sp[2 * r + 1])], axis=1)
        v = whole[local:local + 64]
        bi = 5 * h + i // 2
        st = band[bi]
        keep = ((cols >= st) & (cols < st + BAND)) | ((bi >= starts) & (bi < starts + BAND))
        rows = pl.ds(64 * i, 64)
        sh[rows], sl[rows] = split(jnp.where(keep, v, 0.0))

    @pl.loop(0, 5)
    def _(i):
        rows = pl.ds(pl.multiple_of(i * 128, 128), 128)
        th[rows], tl[rows] = split(dot3(lh[rows], ll[rows], sh[...], sl[...]))

    @pl.when(home)
    def _():
        for r in range(2):
            rows = pl.ds(TILE * r, TILE)
            gh[rows], gl[rows] = split(oblong(lp[2 * r + u]))

    def put(r, v):
        rows = pl.ds(TILE * r, TILE)
        gh[rows], gl[rows] = split(v)

    def chosen(r, unpack, ref):
        a, b = unpack(ref[0]), unpack(ref[1])
        out = []
        for j in range(5):
            sel = assign[p, (5 * r + j) // 2] == 0
            out.append(jnp.where(sel, a[64 * j:64 * j + 64], b[64 * j:64 * j + 64]))
        return jnp.concatenate(out, axis=0)

    @pl.when((u == 2) & (h == 1))
    def _():
        put(0, square(gd[0]))
        put(1, oblong(go[0]))

    @pl.when((u == 3) & (h == 1))
    def _():
        put(0, flipped(go[0]))
        put(1, square(gd[0]))

    @pl.when((u == 2) & (h == 0))
    def _():
        put(0, chosen(0, square, gd))
        put(1, chosen(1, oblong, go))

    @pl.when((u == 3) & (h == 0))
    def _():
        put(0, chosen(0, flipped, go))
        put(1, chosen(1, square, gd))

    for r in range(2):
        rows = pl.ds(TILE * r, TILE)
        v = dot3(th[rows], tl[rows], gh[...], gl[...])
        ch[rows], cl[rows] = split(v)

        @pl.when(c == r)
        def _():
            eye = lax.broadcasted_iota(jnp.int32, (TILE, TILE), 0) == lax.broadcasted_iota(jnp.int32, (TILE, TILE), 1)
            deviation[...] = jnp.where(eye & (2 * h + c == x), 1.0, 0.0) - v

    rows = pl.ds(pl.multiple_of(TILE * c, TILE), TILE)
    corr = dot3(lh[rows], ll[rows], ch[...], cl[...])

    @pl.when(home)
    def _():
        refined[...] = 1.5 * oblong(lp[2 * c + u]) - 0.5 * corr

    @pl.when(u >= 2)
    def _():
        refined[...] = 1.5 * k[...] - 0.5 * corr


def on_device(intersection, children, band_start, assignment):
    s, k = intersection[0], children[0]
    vm = pl.BlockSpec(memory_space=pltpu.VMEM)
    hb = pl.BlockSpec(memory_space=pl.ANY)
    sm = pl.BlockSpec(memory_space=pltpu.SMEM)
    shape = lambda *d: jax.ShapeDtypeStruct(d, F32)
    sp, lp, gd, go = pl.pallas_call(
        gather_kernel,
        out_shape=(shape(4, OFFD, BLK), shape(4, OFFD, BLK), shape(3, DIAG, BLK), shape(2, OFFD, BLK)),
        in_specs=[sm, hb, hb],
        out_specs=(vm, vm, vm, vm),
        scratch_shapes=[
            pltpu.VMEM((TILE, TILE), F32),
            pltpu.VMEM((TILE, TILE), F32),
            pltpu.VMEM((OFFD, BLK), F32),
            pltpu.VMEM((PART, BLK), F32),
            pltpu.SemaphoreType.DMA((2,)),
            pltpu.SemaphoreType.DMA((64,)),
            pltpu.SemaphoreType.DMA((64,)),
        ],
        compiler_params=pltpu.CompilerParams(
            collective_id=0, has_side_effects=True, vmem_limit_bytes=32 << 20
        ),
        name="gather",
    )(assignment, s, k)
    half = lambda n: pltpu.VMEM((HALF, n), BF16)
    refined, deviation = pl.pallas_call(
        multiply_kernel,
        out_shape=(shape(TILE, TILE), shape(TILE, TILE)),
        in_specs=[sm, sm, vm, vm, vm, vm, vm],
        out_specs=(vm, vm),
        scratch_shapes=[half(HALF)] * 6 + [half(TILE)] * 4,
        compiler_params=pltpu.CompilerParams(vmem_limit_bytes=40 << 20),
        name="multiply",
    )(band_start, assignment, k, sp, lp, gd, go)
    return refined[None], deviation[None]


def solution(mesh):
    spec = P("pair", "row", "col")
    return jax.shard_map(
        on_device, mesh=mesh, in_specs=(spec, spec, P(), P()), out_specs=(spec, spec), check_vma=False
    )
```

```python
import jax
import jax.numpy as jnp
from jax import lax
from jax.experimental import pallas as pl
from jax.experimental.pallas import tpu as pltpu
from jax.sharding import PartitionSpec as P

BLK = 128
BAND = 8
TILE = 320
HALF = 640
DIAG = 576
OFFD = 800
PART = 400
MERGES = 32
MESH = pl.DeviceIdType.MESH
F32 = jnp.float32
BF16 = jnp.bfloat16


def place():
    p = lax.axis_index("pair")
    row = lax.axis_index("row")
    x = lax.axis_index("col")
    h, c = row // 2, row % 2
    return p, h, c, x, (x + 2 * h) % 4


def device(p, h, c, u):
    return ((p + MERGES) % MERGES, 2 * h + c, (u + 2 * h) % 4)


def split(v):
    hi = v.astype(BF16)
    return hi, (v - hi.astype(F32)).astype(BF16)


def dot3(ah, al, bh, bl):
    d = lambda a, b: jnp.dot(a, b, preferred_element_type=F32)
    return d(ah, bh) + (d(ah, bl) + d(al, bh))


def pack(ref, v):
    ref[0:320] = v[:, 0:128]
    ref[320:640] = v[:, 128:256]
    ref[640:800] = jnp.concatenate([v[0:160, 256:320], v[160:320, 256:320]], axis=1)


def oblong(v):
    e = v[640:800]
    return jnp.concatenate([v[0:320], v[320:640], jnp.concatenate([e[:, 0:64], e[:, 64:128]], axis=0)], axis=1)


def flipped(v):
    return oblong(v).T


def square(v):
    a, b, e = v[0:320], v[320:512], v[512:576, 0:64]
    r0 = jnp.concatenate([a[0:128], a[128:320].T], axis=1)
    r1 = jnp.concatenate([a[128:256], b[0:128], b[128:192].T], axis=1)
    r2 = jnp.concatenate([a[256:320], b[128:192], e], axis=1)
    return jnp.concatenate([r0, r1, r2], axis=0)


def refine_kernel(
    band, assign, s_hbm, k_hbm, refined, deviation,
    sp, lp, gd, go, s, k, ko, zb, lh, ll, sh, sl, th, tl, wh, wl, gh, gl, yh, yl_, ch, cl, local, send, recv,
):
    p, h, c, x, u = place()
    home = u < 2
    guest = u >= 2
    plane0 = h == 0
    plane1 = h == 1
    high = x >= 2
    diag_home = home & (u == c)
    off_home = home & (u != c)
    relay = guest & (c == 1)
    landing = home & (c == 1)
    holds_diag = c == x % 2
    first_off = jnp.where(home, u, 3 - u) != c
    other = device(p, h, 1 - c, u)
    used = [0]

    def copy(src, dst, to, which=0, ways=1, came=None):
        i = used[0] + which
        used[0] += ways
        return pltpu.make_async_remote_copy(
            src_ref=src, dst_ref=dst, send_sem=send.at[i], recv_sem=recv.at[i if came is None else came],
            device_id=to, device_id_type=MESH,
        )

    def on(cond, *acts):
        @pl.when(cond)
        def _():
            for act in acts:
                act()

    def cut(ref, n, parts):
        return [ref.at[pl.ds(i * (n // parts), n // parts)] for i in range(parts)]

    def copies(src, dst, n, parts, to):
        return [copy(a, b, to) for a, b in zip(cut(src, n, parts), cut(dst, n, parts))]

    load_k = pltpu.make_async_copy(k_hbm, k, local.at[0])
    load_s = pltpu.make_async_copy(s_hbm, s, local.at[1])
    load_k.start()
    load_s.start()
    barrier = pltpu.get_barrier_semaphore()
    friends = [device(p, 1 - h, c, (u + 2) % 4)]
    for q in (p - 1, p + 1):
        friends += [device(q, h, b, v) for v in range(4) for b in range(2)]
    friends += [device(p, h, b, (u + v) % 4) for v in range(4) for b in (c, 1 - c) if v or b is not c]
    for d in friends:
        pl.semaphore_signal(barrier, inc=1, device_id=d, device_id_type=MESH)
    last = (p == MERGES - 1) & plane1
    zeroth = (p == 0) & plane1
    seam = last | zeroth | ((p == 0) & plane0) | ((p == MERGES - 1) & plane0)

    @pl.when(seam)
    def _():
        for b in range(2):
            for v in range(4):
                d = (MERGES - 1 - p, 2 * (1 - h) + b, v)
                pl.semaphore_signal(barrier, inc=1, device_id=d, device_id_type=MESH)

    own_s = 2 * c + u % 2
    far_s = 2 * c + 1 - u % 2
    first = jnp.where(home, 2 * c + u, 2 * c + 3 - u)
    second = jnp.where(home, 2 * c + 1 - u, 2 * c + u - 2)

    load_k.wait()

    @pl.when(diag_home)
    def _():
        gd[2, 0:320] = k[:, 0:128]
        gd[2, 320:512] = k[128:320, 128:256]
        gd[2, 512:576, 0:64] = k[256:320, 256:320]
        gd[2, 512:576, 64:128] = jnp.zeros((64, 64), F32)

    @pl.when(off_home)
    def _():
        pack(ko, k)

    @pl.when(home & plane0)
    def _():
        pack(lp.at[first], k)

    load_s.wait()
    pack(sp.at[own_s], s)

    NZ, NR, NL = 4, 5, 5
    step = PART // NR
    twin = device(p, 1 - h, c, (u + 2) % 4)
    r0 = copies(ko.at[pl.ds(0, PART)], zb, PART, NR, device(p, h, c, 3))
    r1 = copies(ko.at[pl.ds(PART, PART)], zb, PART, NR, device(p, h, c, 2))
    zo = copies(zb, zb, PART, NR, twin)
    zd = copies(gd.at[2], gd.at[jnp.where(plane0, 0, 2)], DIAG, NZ, twin)
    at_r = used[0]
    fr = copies(gd.at[2], gd.at[0], DIAG, NZ, device(p + 1, h, c, u))
    at_l = used[0]
    fl = copies(gd.at[2], gd.at[1], DIAG, NZ, device(p - 1, h, c, u))
    yr = copies(ko, go.at[0], OFFD, NL, device(p + 1, h, c, u))
    yl = copies(ko, go.at[1], OFFD, NL, device(p - 1, h, c, u))
    gs0 = copies(gd.at[0], gd.at[0], DIAG, NZ, other)
    gs1 = copies(gd.at[1], gd.at[1], DIAG, NZ, other)
    part = 1 - x % 2
    begin = pl.multiple_of(part * PART, 8)
    base = jnp.where(high, 0, 2)
    ahead = jnp.where(high, p, p + 1)
    spread = [[[] for _ in range(NR)] for _ in range(2)]
    across = [[[] for _ in range(NR)] for _ in range(2)]
    at_go = used[0]
    for i in range(2):
        for slot, q in ((0, ahead), (1, p - 1)):
            for j in range(NR):
                at = used[0]
                src, dst = zb.at[pl.ds(j * step, step)], go.at[slot, pl.ds(begin + j * step, step)]
                spread[slot][j].append(copy(src, dst, ((q + MERGES) % MERGES, 2 * h + 1 - i, base + i), part, 2))
                to = (MERGES - 1 - p, 1 - i, 2 + i)
                across[slot][j].append(copy(src, dst, to, came=at + part))

    def landed(slot, n, j):
        i = at_go + (slot * NR + j) * 3 + n + (x % 2) * (2 * NR * 3)
        return pltpu.make_async_remote_copy(
            src_ref=zb.at[pl.ds(0, step)], dst_ref=go.at[slot, pl.ds(n * PART + j * step, step)],
            send_sem=send.at[i], recv_sem=recv.at[i], device_id=other, device_id_type=MESH,
        )

    came = [[[landed(slot, n, j) for j in range(NR)] for n in range(2)] for slot in range(2)]
    sr = [copy(a, b, (MERGES - 1 - p, c, x), came=at_r + i) for i, (a, b) in enumerate(zip(cut(gd.at[2], DIAG, NZ), cut(gd.at[0], DIAG, NZ)))]
    sw = [copy(a, b, (MERGES - 1 - p, c, x), came=at_l + i) for i, (a, b) in enumerate(zip(cut(gd.at[2], DIAG, NZ), cut(gd.at[1], DIAG, NZ)))]
    os0 = copies(go.at[0], go.at[0], OFFD, 2, other)
    os1 = copies(go.at[1], go.at[1], OFFD, 2, other)
    sx = copy(sp.at[own_s], sp.at[own_s], device(p, h, c, u + 1 - 2 * (u % 2)))
    sc0 = copy(sp.at[own_s], sp.at[own_s], other)
    sc1 = copy(sp.at[far_s], sp.at[far_s], other)
    hh = copy(lp.at[first], lp.at[first], device(p, h, c, 1 - u))
    hg = copies(lp.at[first], lp.at[first], OFFD, NL, device(p, h, c, 3 - u))
    gg = copies(lp.at[first], lp.at[first], OFFD, NL, device(p, h, c, 5 - u))
    ca = copy(lp.at[first], lp.at[first], other)
    cb = copy(lp.at[second], lp.at[second], other)

    starts = lambda cs: [d.start for d in cs]
    arrives = lambda cs: [d.wait_recv for d in cs]
    leaves = lambda cs: [d.wait_send for d in cs]
    both = lambda a, b: [d for pair in zip(a, b) for d in pair]
    flat = lambda a: [d for b in a for d in b]

    pl.semaphore_wait(barrier, len(friends) + 8 * seam.astype(jnp.int32))

    on(off_home & (u == 0), *starts(both(r0, r1)))
    on(diag_home, *starts(zd))
    on(diag_home & plane1, *starts(both(fr, fl)))
    on(diag_home & last, *starts(sr))
    on(diag_home & zeroth, *starts(sw))
    on(off_home & plane1, *starts(both(yr, yl)))
    on(home & plane0, *starts(hg), ca.start)
    on(diag_home & plane0, hh.start)
    on(guest | diag_home, sx.start)
    sc0.start()

    for j in range(NR):
        on(relay & (u == 3), r0[j].wait_recv)
        on(relay & (u == 2), r1[j].wait_recv)
        on(relay, zo[j].start)
        on(relay & last, *starts(across[0][j]))
        on(relay & zeroth, *starts(across[1][j]))

    def pick(row, a, b):
        return jnp.where(assign[(5 * c + row // 64) // 2, p] == 0, a, b)

    @pl.when(diag_home & plane1)
    def _():
        for d in fr + fl:
            d.wait_recv()
        a, b = square(gd[0]), square(gd[1])
        pack(lp.at[first], jnp.concatenate([pick(i, a[i:i + 64], b[i:i + 64]) for i in range(0, 320, 64)], axis=0))
        for d in hg + [hh, ca]:
            d.start()

    @pl.when(off_home & plane1)
    def _():
        edges = ((0, 64, 128, 160), (160, 192, 256, 320))
        for j in range(NL):
            yr[j].wait_recv()
            yl[j].wait_recv()
            if j < 4:
                e = edges[j % 2]
                for lo, hi in zip(e, e[1:]):
                    at = pl.ds(320 * (j // 2) + lo, hi - lo)
                    lp[first, at] = pick(lo, go[0, at], go[1, at])
            else:
                for lo, hi in ((0, 32), (32, 64), (64, 96), (96, 128), (128, 160)):
                    at = pl.ds(640 + lo, hi - lo)
                    a, b = go[0, at], go[1, at]
                    lp[first, at] = jnp.concatenate(
                        [pick(lo, a[:, 0:64], b[:, 0:64]), pick(160 + lo, a[:, 64:128], b[:, 64:128])], axis=1
                    )
            hg[j].start()
        hh.start()
        ca.start()

    on(guest | off_home, sx.wait_recv, sc1.start)

    for j in range(NL):
        on(guest, hg[j].wait_recv)
        on(guest & (plane1 | ~first_off), gg[j].start)
    on(guest, ca.start)
    on(guest & plane0 & first_off, *arrives(gg), cb.start)
    on(off_home & plane0, hh.wait_recv, cb.start)

    for j in range(NZ):
        on(guest & plane0 & holds_diag, zd[j].wait_recv)
        on(guest & plane0 & holds_diag & (p < MERGES - 1), fr[j].start)
        on(guest & plane0 & holds_diag & (p > 0), fl[j].start)
        on(guest & plane1 & holds_diag, zd[j].wait_recv, gs0[j].start)
    for j in range(NR):
        on(landing, zo[j].wait_recv)
        on(landing & (plane1 | (p < MERGES - 1)), *starts(spread[0][j]))
        on(landing & plane0 & (p > 0), *starts(spread[1][j]))
    on(home & plane1, hh.wait_recv, cb.start)

    sc0.wait_recv()
    on(guest | diag_home, sc1.wait_recv)

    @pl.when(home)
    def _():
        pack(sp.at[1 + u], flipped(sp[2 - u]))

    hc = x // 2
    cols = lax.broadcasted_iota(jnp.int32, (1, HALF), 1) // BLK
    begins = jnp.zeros((1, HALF), jnp.int32)
    for j in range(5):
        begins = jnp.where(cols == j, band[5 * hc + j], begins)
    cols = cols + 5 * hc
    for r in range(2):
        whole = jnp.concatenate([oblong(sp[2 * r]), oblong(sp[2 * r + 1])], axis=1)
        for i in range(5):
            bi = 5 * h + (5 * r + i) // 2
            st = band[bi]
            keep = ((cols >= st) & (cols < st + BAND)) | ((bi >= begins) & (bi < begins + BAND))
            rows = pl.ds(TILE * r + 64 * i, 64)
            sh[rows], sl[rows] = split(jnp.where(keep, whole[64 * i:64 * i + 64], 0.0))

    def left():
        @pl.when(plane0)
        def _():
            @pl.when((u == 0) | (u == 3))
            def _():
                pack(lp.at[1], flipped(lp[2]))

            @pl.when((u == 1) | (u == 2))
            def _():
                pack(lp.at[2], flipped(lp[1]))

        for r in range(2):
            rows = pl.ds(TILE * r, TILE)
            lh[rows], ll[rows] = split(jnp.concatenate([oblong(lp[2 * r]), oblong(lp[2 * r + 1])], axis=1))

    def right(r, v):
        rows = pl.ds(TILE * r, TILE)
        gh[rows], gl[rows] = split(v)

    def store_deviation(v):
        eye = lax.broadcasted_iota(jnp.int32, (TILE, TILE), 0) == lax.broadcasted_iota(jnp.int32, (TILE, TILE), 1)
        deviation[...] = jnp.where(eye & (2 * h + c == x), 1.0, 0.0) - v

    own_rows = pl.ds(pl.multiple_of(TILE * c, 64), TILE)

    def values_times_right():
        @pl.loop(0, 5)
        def _(i):
            rows = pl.ds(pl.multiple_of(i * 128, 128), 128)
            yh[rows], yl_[rows] = split(dot3(sh[rows], sl[rows], gh[...], gl[...]))

    def left_times_that():
        for r in range(2):
            rows = pl.ds(TILE * r, TILE)
            v = dot3(lh[rows], ll[rows], yh[...], yl_[...])
            ch[rows], cl[rows] = split(v)

            @pl.when(c == r)
            def _():
                store_deviation(v)

        return dot3(lh[own_rows], ll[own_rows], ch[...], cl[...])

    @pl.when(guest & plane0)
    def _():
        ca.wait_recv()

        @pl.when(~first_off)
        def _():
            cb.wait_recv()

        left()

        @pl.loop(0, 5)
        def _(i):
            rows = pl.ds(pl.multiple_of(i * 128, 128), 128)
            th[rows], tl[rows] = split(dot3(lh[rows], ll[rows], sh[...], sl[...]))

        wh[0:320], wl[0:320] = th[own_rows], tl[own_rows]
        for i in range(2):
            rows = pl.ds(pl.multiple_of(TILE * c + 160 * i, 32), 160)
            at = pl.ds(320 + 160 * i, 160)
            wh[at], wl[at] = split(dot3(lh[rows], ll[rows], th[...], tl[...]))

    on(guest & plane0 & holds_diag, *[a for j in range(NZ) for a in (fr[j].wait_recv, gs0[j].start, fl[j].wait_recv, gs1[j].start)])
    for n in range(2):
        on(guest & ~holds_diag, *arrives(came[0][n]), os0[n].start)
        on(guest & plane0 & ~holds_diag, *arrives(came[1][n]), os1[n].start)
    on(guest & ~holds_diag, *arrives(gs0))
    on(guest & ~holds_diag & plane0, *arrives(gs1))
    on(guest & holds_diag, *arrives(os0))
    on(guest & holds_diag & plane0, *arrives(os1))

    def chosen(r, unpack, ref):
        a, b = unpack(ref[0]), unpack(ref[1])
        out = []
        for j in range(5):
            sel = assign[(5 * r + j) // 2, p] == 0
            out.append(jnp.where(sel, a[64 * j:64 * j + 64], b[64 * j:64 * j + 64]))
        return jnp.concatenate(out, axis=0)

    @pl.when(guest & plane0)
    def _():
        @pl.when(u == 2)
        def _():
            right(0, chosen(0, square, gd))
            right(1, chosen(1, oblong, go))

        @pl.when(u == 3)
        def _():
            right(0, chosen(0, flipped, go))
            right(1, chosen(1, square, gd))

        store_deviation(dot3(wh[0:320], wl[0:320], gh[...], gl[...]))
        refined[...] = 1.5 * k[...] - 0.5 * dot3(wh[320:640], wl[320:640], gh[...], gl[...])

    @pl.when(guest & plane1)
    def _():
        @pl.when(u == 2)
        def _():
            right(0, square(gd[0]))
            right(1, oblong(go[0]))

        @pl.when(u == 3)
        def _():
            right(0, flipped(go[0]))
            right(1, square(gd[0]))

        values_times_right()
        for d in gg:
            d.wait_recv()
        cb.start()
        ca.wait_recv()
        cb.wait_recv()
        left()
        refined[...] = 1.5 * k[...] - 0.5 * left_times_that()

    @pl.when(home)
    def _():
        ca.wait_recv()

        @pl.when(plane1 | (u == c))
        def _():
            cb.wait_recv()

        left()
        for r in range(2):
            right(r, oblong(lp[2 * r + u]))
        values_times_right()
        refined[...] = 1.5 * oblong(lp[2 * c + u]) - 0.5 * left_times_that()

    sc0.wait_send()
    ca.wait_send()
    on(guest | diag_home, sx.wait_send)
    on(guest | off_home, sc1.wait_send)
    on(plane1 | first_off, cb.wait_send)
    on(home & (plane1 | ~first_off), hh.wait_send)
    on(home, *leaves(hg))
    on(guest & (plane1 | ~first_off), *leaves(gg))
    on(diag_home, *leaves(zd))
    on(diag_home & plane1, *leaves(fr + fl))
    on(diag_home & last, *leaves(sr))
    on(diag_home & zeroth, *leaves(sw))
    on(guest & plane0 & holds_diag & (p < MERGES - 1), *leaves(fr))
    on(guest & plane0 & holds_diag & (p > 0), *leaves(fl))
    on(off_home & plane1, *leaves(yr + yl))
    on(off_home & (u == 0), *leaves(r0 + r1))
    on(relay, *leaves(zo))
    on(relay & last, *leaves(flat(across[0])))
    on(relay & zeroth, *leaves(flat(across[1])))
    on(landing & (plane1 | (p < MERGES - 1)), *leaves(flat(spread[0])))
    on(landing & plane0 & (p > 0), *leaves(flat(spread[1])))
    on(guest & ~holds_diag, *leaves(os0))
    on(guest & ~holds_diag & plane0, *leaves(os1))
    on(guest & holds_diag, *leaves(gs0))
    on(guest & holds_diag & plane0, *leaves(gs1))


def on_device(intersection, children, band_start, assignment):
    s, k = intersection[0], children[0]
    vm = pl.BlockSpec(memory_space=pltpu.VMEM)
    sm = pl.BlockSpec(memory_space=pltpu.SMEM)
    hb = pl.BlockSpec(memory_space=pltpu.HBM)
    shape = jax.ShapeDtypeStruct((TILE, TILE), F32)
    vmem = lambda *d: pltpu.VMEM(d, F32)
    half = lambda n: pltpu.VMEM((HALF, n), BF16)
    refined, deviation = pl.pallas_call(
        refine_kernel,
        out_shape=(shape, shape),
        in_specs=[sm, sm, hb, hb],
        out_specs=(vm, vm),
        scratch_shapes=[
            vmem(4, OFFD, BLK), vmem(4, OFFD, BLK), vmem(3, DIAG, BLK), vmem(2, OFFD, BLK),
            vmem(TILE, TILE), vmem(TILE, TILE), vmem(OFFD, BLK), vmem(PART, BLK),
        ]
        + [half(HALF)] * 8
        + [half(TILE)] * 6
        + [
            pltpu.SemaphoreType.DMA((2,)),
            pltpu.SemaphoreType.DMA((160,)),
            pltpu.SemaphoreType.DMA((160,)),
        ],
        compiler_params=pltpu.CompilerParams(
            collective_id=0, has_side_effects=True, vmem_limit_bytes=48 << 20
        ),
        name="refine",
    )(band_start, assignment.T, s, k)
    return refined[None], deviation[None]


def solution(mesh):
    spec = P("pair", "row", "col")
    return jax.shard_map(
        on_device, mesh=mesh, in_specs=(spec, spec, P(), P()), out_specs=(spec, spec), check_vma=False
    )
```

```python
import jax
import jax.numpy as jnp
from jax import lax
from jax.experimental import pallas as pl
from jax.experimental.pallas import tpu as pltpu
from jax.sharding import PartitionSpec as P

BLK = 128
BAND = 8
TILE = 320
HALF = 640
DIAG = 576
OFFD = 800
PART = 400
MERGES = 32
MESH = pl.DeviceIdType.MESH
F32 = jnp.float32
BF16 = jnp.bfloat16


def place():
    p = lax.axis_index("pair")
    row = lax.axis_index("row")
    x = lax.axis_index("col")
    h, c = row // 2, row % 2
    return p, h, c, x, (x + 2 * h) % 4


def device(p, h, c, u):
    return ((p + MERGES) % MERGES, 2 * h + c, (u + 2 * h) % 4)


def split(v):
    hi = v.astype(BF16)
    return hi, (v - hi.astype(F32)).astype(BF16)


def dot3(ah, al, bh, bl):
    d = lambda a, b: jnp.dot(a, b, preferred_element_type=F32)
    return d(ah, bh) + (d(ah, bl) + d(al, bh))


def pack(ref, v):
    ref[0:320] = v[:, 0:128]
    ref[320:640] = v[:, 128:256]
    ref[640:800] = jnp.concatenate([v[0:160, 256:320], v[160:320, 256:320]], axis=1)


def oblong(v):
    e = v[640:800]
    return jnp.concatenate([v[0:320], v[320:640], jnp.concatenate([e[:, 0:64], e[:, 64:128]], axis=0)], axis=1)


def flipped(v):
    return oblong(v).T


def square(v):
    a, b, e = v[0:320], v[320:512], v[512:576, 0:64]
    r0 = jnp.concatenate([a[0:128], a[128:320].T], axis=1)
    r1 = jnp.concatenate([a[128:256], b[0:128], b[128:192].T], axis=1)
    r2 = jnp.concatenate([a[256:320], b[128:192], e], axis=1)
    return jnp.concatenate([r0, r1, r2], axis=0)


def refine_kernel(
    band, assign, s_hbm, k_hbm, refined, deviation,
    sp, lp, gd, go, s, k, ko, zb, zn, zs, lh, ll, sh, sl, th, tl, wh, wl, gh, gl, yh, yl_, ch, cl, local, send, recv,
):
    p, h, c, x, u = place()
    home = u < 2
    guest = u >= 2
    plane0 = h == 0
    plane1 = h == 1
    high = x >= 2
    diag_home = home & (u == c)
    off_home = home & (u != c)
    relay = guest & (c == 1)
    landing = home & (c == 1)
    holds_diag = c == x % 2
    first_off = jnp.where(home, u, 3 - u) != c
    other = device(p, h, 1 - c, u)
    used = [0]

    def copy(src, dst, to, which=0, ways=1, came=None):
        i = used[0] + which
        used[0] += ways
        return pltpu.make_async_remote_copy(
            src_ref=src, dst_ref=dst, send_sem=send.at[i], recv_sem=recv.at[i if came is None else came],
            device_id=to, device_id_type=MESH,
        )

    def on(cond, *acts):
        @pl.when(cond)
        def _():
            for act in acts:
                act()

    def cut(ref, n, parts):
        return [ref.at[pl.ds(i * (n // parts), n // parts)] for i in range(parts)]

    def copies(src, dst, n, parts, to):
        return [copy(a, b, to) for a, b in zip(cut(src, n, parts), cut(dst, n, parts))]

    load_k = pltpu.make_async_copy(k_hbm, k, local.at[0])
    load_s = pltpu.make_async_copy(s_hbm, s, local.at[1])
    load_k.start()
    load_s.start()
    barrier = pltpu.get_barrier_semaphore()
    friends = [device(p, 1 - h, c, (u + 2) % 4)]
    for q in (p - 1, p + 1):
        friends += [device(q, h, b, v) for v in range(4) for b in range(2)]
    friends += [device(p, h, b, (u + v) % 4) for v in range(4) for b in (c, 1 - c) if v or b is not c]
    for d in friends:
        pl.semaphore_signal(barrier, inc=1, device_id=d, device_id_type=MESH)
    last = (p == MERGES - 1) & plane1
    zeroth = (p == 0) & plane1
    seam = last | zeroth | ((p == 0) & plane0) | ((p == MERGES - 1) & plane0)

    @pl.when(seam)
    def _():
        for b in range(2):
            for v in range(4):
                d = (MERGES - 1 - p, 2 * (1 - h) + b, v)
                pl.semaphore_signal(barrier, inc=1, device_id=d, device_id_type=MESH)

    own_s = 2 * c + u % 2
    far_s = 2 * c + 1 - u % 2
    first = jnp.where(home, 2 * c + u, 2 * c + 3 - u)
    second = jnp.where(home, 2 * c + 1 - u, 2 * c + u - 2)

    load_k.wait()

    @pl.when(diag_home)
    def _():
        gd[2, 0:320] = k[:, 0:128]
        gd[2, 320:512] = k[128:320, 128:256]
        gd[2, 512:576, 0:64] = k[256:320, 256:320]
        gd[2, 512:576, 64:128] = jnp.zeros((64, 64), F32)

    @pl.when(off_home)
    def _():
        pack(ko, k)

    @pl.when(home & plane0)
    def _():
        pack(lp.at[first], k)

    load_s.wait()
    pack(sp.at[own_s], s)

    NZ, NR, NL = 4, 5, 5
    step = PART // NR
    twin = device(p, 1 - h, c, (u + 2) % 4)
    r0 = copies(ko.at[pl.ds(0, PART)], zb, PART, NR, device(p, h, c, 3))
    r1 = copies(ko.at[pl.ds(PART, PART)], zb, PART, NR, device(p, h, c, 2))
    zo = copies(zb, zb, PART, NR, twin)
    zd = copies(gd.at[2], gd.at[jnp.where(plane0, 0, 2)], DIAG, NZ, twin)
    at_r = used[0]
    fr = copies(gd.at[2], gd.at[0], DIAG, NZ, device(p + 1, h, c, u))
    at_l = used[0]
    fl = copies(gd.at[2], gd.at[1], DIAG, NZ, device(p - 1, h, c, u))
    yr = copies(ko, go.at[0], OFFD, NL, device(p + 1, h, c, u))
    yl = copies(ko, go.at[1], OFFD, NL, device(p - 1, h, c, u))
    gs0 = copies(gd.at[0], gd.at[0], DIAG, NZ, other)
    gs1 = copies(gd.at[1], gd.at[1], DIAG, NZ, other)
    part = 1 - x % 2
    begin = pl.multiple_of(part * PART, 8)
    base = jnp.where(high, 0, 2)
    at_n = used[0]
    nr = copies(zb, zn.at[0], PART, NR, device(p + 1, h, c, u))
    nl = copies(zb, zn.at[1], PART, NR, device(p - 1, h, c, u))
    seam_r = [copy(a, b, (MERGES - 1 - p, c, x), came=at_n + i) for i, (a, b) in enumerate(zip(cut(zb, PART, NR), cut(zn.at[0], PART, NR)))]
    seam_l = [copy(a, b, (MERGES - 1 - p, c, x), came=at_n + NR + i) for i, (a, b) in enumerate(zip(cut(zb, PART, NR), cut(zn.at[1], PART, NR)))]
    spread = [[] for _ in range(NR)]
    chosen_spread = [[] for _ in range(NR)]
    at_go = used[0]
    for i in range(2):
        for j in range(NR):
            at = used[0]
            rows, dst = pl.ds(j * step, step), go.at[0, pl.ds(begin + j * step, step)]
            to = (p, 2 * h + 1 - i, base + i)
            spread[j].append(copy(zb.at[rows], dst, to, part, 2))
            used[0] = at
            chosen_spread[j].append(copy(zs.at[i, rows], dst, to, part, 2))

    def landed(n, j):
        i = at_go + j * 2 + n + (x % 2) * (2 * NR)
        return pltpu.make_async_remote_copy(
            src_ref=zb.at[pl.ds(0, step)], dst_ref=go.at[0, pl.ds(n * PART + j * step, step)],
            send_sem=send.at[i], recv_sem=recv.at[i], device_id=other, device_id_type=MESH,
        )

    came = [[landed(n, j) for j in range(NR)] for n in range(2)]
    sr = [copy(a, b, (MERGES - 1 - p, c, x), came=at_r + i) for i, (a, b) in enumerate(zip(cut(gd.at[2], DIAG, NZ), cut(gd.at[0], DIAG, NZ)))]
    sw = [copy(a, b, (MERGES - 1 - p, c, x), came=at_l + i) for i, (a, b) in enumerate(zip(cut(gd.at[2], DIAG, NZ), cut(gd.at[1], DIAG, NZ)))]
    os0 = copies(go.at[0], go.at[0], OFFD, 2, other)
    sx = copy(sp.at[own_s], sp.at[own_s], device(p, h, c, u + 1 - 2 * (u % 2)))
    sc0 = copy(sp.at[own_s], sp.at[own_s], other)
    sc1 = copy(sp.at[far_s], sp.at[far_s], other)
    hh = copies(lp.at[first], lp.at[first], OFFD, NL, device(p, h, c, 1 - u))
    hg = copies(lp.at[first], lp.at[first], OFFD, NL, device(p, h, c, 3 - u))
    gg = copies(lp.at[first], lp.at[first], OFFD, NL, device(p, h, c, 5 - u))[:3]
    hf = copies(lp.at[second], lp.at[second], OFFD, NL, device(p, h, c, 3 - u))[3:]
    ca = copy(lp.at[first], lp.at[first], other)
    cb = copy(lp.at[second], lp.at[second], other)

    starts = lambda cs: [d.start for d in cs]
    arrives = lambda cs: [d.wait_recv for d in cs]
    leaves = lambda cs: [d.wait_send for d in cs]
    both = lambda a, b: [d for pair in zip(a, b) for d in pair]
    flat = lambda a: [d for b in a for d in b]

    pl.semaphore_wait(barrier, len(friends) + 8 * seam.astype(jnp.int32))

    on(off_home & (u == 0), *starts(both(r0, r1)))
    y = p % 4
    on(diag_home & plane1, *starts(both(fr, fl)))
    on(diag_home & last, *starts(sr))
    on(diag_home & zeroth, *starts(sw))
    on(diag_home, *starts(zd))
    on(off_home & plane1, *starts(both(yr, yl)))
    on(home & plane0, *starts(hg), ca.start)
    on(diag_home & plane0, *starts(hh))
    on(guest | diag_home, sx.start)
    sc0.start()

    late = plane0 & ((y == 0) | (y == 3))
    for j in range(NR):
        on(relay & (u == 3), r0[j].wait_recv)
        on(relay & (u == 2), r1[j].wait_recv)
        on(relay & ~late, zo[j].start)
        on(relay & last, seam_r[j].start)
        on(relay & zeroth, seam_l[j].start)

    def pick(row, a, b):
        return jnp.where(assign[(5 * c + row // 64) // 2, p] == 0, a, b)

    @pl.when(diag_home & plane1)
    def _():
        for d in fr + fl:
            d.wait_recv()
        a, b = square(gd[0]), square(gd[1])
        pack(lp.at[first], jnp.concatenate([pick(i, a[i:i + 64], b[i:i + 64]) for i in range(0, 320, 64)], axis=0))
        for d in both(hg, hh) + [ca]:
            d.start()

    @pl.when(off_home & plane1)
    def _():
        edges = ((0, 64, 128, 160), (160, 192, 256, 320))
        for j in range(NL):
            yr[j].wait_recv()
            yl[j].wait_recv()
            if j < 4:
                e = edges[j % 2]
                for lo, hi in zip(e, e[1:]):
                    at = pl.ds(320 * (j // 2) + lo, hi - lo)
                    lp[first, at] = pick(lo, go[0, at], go[1, at])
            else:
                for lo, hi in ((0, 32), (32, 64), (64, 96), (96, 128), (128, 160)):
                    at = pl.ds(640 + lo, hi - lo)
                    a, b = go[0, at], go[1, at]
                    lp[first, at] = jnp.concatenate(
                        [pick(lo, a[:, 0:64], b[:, 0:64]), pick(160 + lo, a[:, 64:128], b[:, 64:128])], axis=1
                    )
            hg[j].start()
            hh[j].start()
        ca.start()

    on(guest | off_home, sx.wait_recv, sc1.start)

    for j in range(NL):
        on(guest, hg[j].wait_recv)
        if j < len(gg):
            on(guest & (plane1 | ~first_off), gg[j].start)
    on(relay & late, *starts(zo))
    on(guest, ca.start)
    on(home & (plane1 | first_off), *arrives(hh[3:]), *starts(hf), *arrives(hh[:3]), cb.start)
    on(guest & plane0 & first_off, *arrives(gg + hf), cb.start)

    for j in range(NZ):
        on(guest & plane0 & holds_diag, zd[j].wait_recv)
        on(guest & plane0 & holds_diag & (p < MERGES - 1), fr[j].start)
        on(guest & plane0 & holds_diag & (p > 0), fl[j].start)
        on(guest & plane1 & holds_diag, zd[j].wait_recv, gs0[j].start)
    for j in range(NR):
        on(landing, zo[j].wait_recv)
        on(landing & plane1, *starts(spread[j]))
        on(landing & plane0 & (p < MERGES - 1), nr[j].start)
        on(landing & plane0 & (p > 0), nl[j].start)

    @pl.when(landing & plane0)
    def _():
        lanes = lax.broadcasted_iota(jnp.int32, (16, BLK), 1)
        for j in range(NR):
            nr[j].wait_recv()
            nl[j].wait_recv()
            for g in range(step // 16):
                row = begin + j * step + g * 16
                slab, t = row // TILE, row % TILE
                low = assign[(5 + t // 64) // 2, p]
                up = assign[(5 + (t + 160 * (slab // 2)) // 64) // 2, p]
                at = pl.ds(j * step + g * 16, 16)
                a, b = zn[0, at], zn[1, at]
                zs[0, at] = jnp.where(jnp.where(lanes < 64, low, up) == 0, a, b)
                zs[1, at] = jnp.where(assign[slab, p] == 0, a, b)
            for d in chosen_spread[j]:
                d.start()

    sc0.wait_recv()
    on(guest | diag_home, sc1.wait_recv)

    @pl.when(home)
    def _():
        pack(sp.at[1 + u], flipped(sp[2 - u]))

    hc = x // 2
    cols = lax.broadcasted_iota(jnp.int32, (1, HALF), 1) // BLK
    begins = jnp.zeros((1, HALF), jnp.int32)
    for j in range(5):
        begins = jnp.where(cols == j, band[5 * hc + j], begins)
    cols = cols + 5 * hc
    for r in range(2):
        whole = jnp.concatenate([oblong(sp[2 * r]), oblong(sp[2 * r + 1])], axis=1)
        for i in range(5):
            bi = 5 * h + (5 * r + i) // 2
            st = band[bi]
            keep = ((cols >= st) & (cols < st + BAND)) | ((bi >= begins) & (bi < begins + BAND))
            rows = pl.ds(TILE * r + 64 * i, 64)
            sh[rows], sl[rows] = split(jnp.where(keep, whole[64 * i:64 * i + 64], 0.0))

    def left():
        @pl.when(plane0)
        def _():
            @pl.when((u == 0) | (u == 3))
            def _():
                pack(lp.at[1], flipped(lp[2]))

            @pl.when((u == 1) | (u == 2))
            def _():
                pack(lp.at[2], flipped(lp[1]))

        for r in range(2):
            rows = pl.ds(TILE * r, TILE)
            lh[rows], ll[rows] = split(jnp.concatenate([oblong(lp[2 * r]), oblong(lp[2 * r + 1])], axis=1))

    def right(r, v):
        rows = pl.ds(TILE * r, TILE)
        gh[rows], gl[rows] = split(v)

    def store_deviation(v):
        eye = lax.broadcasted_iota(jnp.int32, (TILE, TILE), 0) == lax.broadcasted_iota(jnp.int32, (TILE, TILE), 1)
        deviation[...] = jnp.where(eye & (2 * h + c == x), 1.0, 0.0) - v

    own_rows = pl.ds(pl.multiple_of(TILE * c, 64), TILE)

    def values_times_right():
        @pl.loop(0, 5)
        def _(i):
            rows = pl.ds(pl.multiple_of(i * 128, 128), 128)
            yh[rows], yl_[rows] = split(dot3(sh[rows], sl[rows], gh[...], gl[...]))

    def left_times_that():
        for r in range(2):
            rows = pl.ds(TILE * r, TILE)
            v = dot3(lh[rows], ll[rows], yh[...], yl_[...])
            ch[rows], cl[rows] = split(v)

            @pl.when(c == r)
            def _():
                store_deviation(v)

        return dot3(lh[own_rows], ll[own_rows], ch[...], cl[...])

    @pl.when(guest & plane0)
    def _():
        ca.wait_recv()

        @pl.when(~first_off)
        def _():
            cb.wait_recv()

        left()

        @pl.loop(0, 5)
        def _(i):
            rows = pl.ds(pl.multiple_of(i * 128, 128), 128)
            th[rows], tl[rows] = split(dot3(lh[rows], ll[rows], sh[...], sl[...]))

        wh[0:320], wl[0:320] = th[own_rows], tl[own_rows]
        for i in range(2):
            rows = pl.ds(pl.multiple_of(TILE * c + 160 * i, 32), 160)
            at = pl.ds(320 + 160 * i, 160)
            wh[at], wl[at] = split(dot3(lh[rows], ll[rows], th[...], tl[...]))

    on(guest & plane0 & holds_diag, *[a for j in range(NZ) for a in (fr[j].wait_recv, gs0[j].start, fl[j].wait_recv, gs1[j].start)])
    for n in range(2):
        on(guest & ~holds_diag, *arrives(came[n]), os0[n].start)
    on(guest & ~holds_diag, *arrives(gs0))
    on(guest & ~holds_diag & plane0, *arrives(gs1))
    on(guest & holds_diag, *arrives(os0))

    def chosen(r, unpack, ref):
        a, b = unpack(ref[0]), unpack(ref[1])
        out = []
        for j in range(5):
            sel = assign[(5 * r + j) // 2, p] == 0
            out.append(jnp.where(sel, a[64 * j:64 * j + 64], b[64 * j:64 * j + 64]))
        return jnp.concatenate(out, axis=0)

    @pl.when(guest & plane0)
    def _():
        @pl.when(u == 2)
        def _():
            right(0, chosen(0, square, gd))
            right(1, oblong(go[0]))

        @pl.when(u == 3)
        def _():
            right(0, flipped(go[0]))
            right(1, chosen(1, square, gd))

        store_deviation(dot3(wh[0:320], wl[0:320], gh[...], gl[...]))
        refined[...] = 1.5 * k[...] - 0.5 * dot3(wh[320:640], wl[320:640], gh[...], gl[...])

    @pl.when(guest & plane1)
    def _():
        @pl.when(u == 2)
        def _():
            right(0, square(gd[0]))
            right(1, oblong(go[0]))

        @pl.when(u == 3)
        def _():
            right(0, flipped(go[0]))
            right(1, square(gd[0]))

        values_times_right()
        for d in gg + hf:
            d.wait_recv()
        cb.start()
        ca.wait_recv()
        cb.wait_recv()
        left()
        refined[...] = 1.5 * k[...] - 0.5 * left_times_that()

    @pl.when(home)
    def _():
        ca.wait_recv()

        @pl.when(plane1 | (u == c))
        def _():
            cb.wait_recv()

        left()
        for r in range(2):
            right(r, oblong(lp[2 * r + u]))
        values_times_right()
        refined[...] = 1.5 * oblong(lp[2 * c + u]) - 0.5 * left_times_that()

    sc0.wait_send()
    ca.wait_send()
    on(guest | diag_home, sx.wait_send)
    on(guest | off_home, sc1.wait_send)
    on(plane1 | first_off, cb.wait_send)
    on(home & (plane1 | ~first_off), *leaves(hh))
    on(home & (plane1 | first_off), *leaves(hf))
    on(home, *leaves(hg))
    on(guest & (plane1 | ~first_off), *leaves(gg))
    on(diag_home, *leaves(zd))
    on(diag_home & plane1, *leaves(fr + fl))
    on(diag_home & last, *leaves(sr))
    on(diag_home & zeroth, *leaves(sw))
    on(guest & plane0 & holds_diag & (p < MERGES - 1), *leaves(fr))
    on(guest & plane0 & holds_diag & (p > 0), *leaves(fl))
    on(off_home & plane1, *leaves(yr + yl))
    on(off_home & (u == 0), *leaves(r0 + r1))
    on(relay, *leaves(zo))
    on(relay & last, *leaves(seam_r))
    on(relay & zeroth, *leaves(seam_l))
    on(landing & plane1, *leaves(flat(spread)))
    on(landing & plane0, *leaves(flat(chosen_spread)))
    on(landing & plane0 & (p < MERGES - 1), *leaves(nr))
    on(landing & plane0 & (p > 0), *leaves(nl))
    on(guest & ~holds_diag, *leaves(os0))
    on(guest & holds_diag, *leaves(gs0))
    on(guest & holds_diag & plane0, *leaves(gs1))


def on_device(intersection, children, band_start, assignment):
    s, k = intersection[0], children[0]
    vm = pl.BlockSpec(memory_space=pltpu.VMEM)
    sm = pl.BlockSpec(memory_space=pltpu.SMEM)
    hb = pl.BlockSpec(memory_space=pltpu.HBM)
    shape = jax.ShapeDtypeStruct((TILE, TILE), F32)
    vmem = lambda *d: pltpu.VMEM(d, F32)
    half = lambda n: pltpu.VMEM((HALF, n), BF16)
    refined, deviation = pl.pallas_call(
        refine_kernel,
        out_shape=(shape, shape),
        in_specs=[sm, sm, hb, hb],
        out_specs=(vm, vm),
        scratch_shapes=[
            vmem(4, OFFD, BLK), vmem(4, OFFD, BLK), vmem(3, DIAG, BLK), vmem(2, OFFD, BLK),
            vmem(TILE, TILE), vmem(TILE, TILE), vmem(OFFD, BLK), vmem(PART, BLK), vmem(2, PART, BLK), vmem(2, PART, BLK),
        ]
        + [half(HALF)] * 8
        + [half(TILE)] * 6
        + [
            pltpu.SemaphoreType.DMA((2,)),
            pltpu.SemaphoreType.DMA((160,)),
            pltpu.SemaphoreType.DMA((160,)),
        ],
        compiler_params=pltpu.CompilerParams(
            collective_id=0, has_side_effects=True, vmem_limit_bytes=62 << 20
        ),
        name="refine",
    )(band_start, assignment.T, s, k)
    return refined[None], deviation[None]


def solution(mesh):
    spec = P("pair", "row", "col")
    return jax.shard_map(
        on_device, mesh=mesh, in_specs=(spec, spec, P(), P()), out_specs=(spec, spec), check_vma=False
    )
```

```python
import jax
import jax.numpy as jnp
from jax import lax
from jax.experimental import pallas as pl
from jax.experimental.pallas import tpu as pltpu
from jax.sharding import PartitionSpec as P

BLK = 128
BAND = 8
TILE = 320
HALF = 640
DIAG = 456
OFFD = 800
PART = 400
MERGES = 32
MESH = pl.DeviceIdType.MESH
F32 = jnp.float32
BF16 = jnp.bfloat16


def place():
    p = lax.axis_index("pair")
    row = lax.axis_index("row")
    x = lax.axis_index("col")
    h, c = row // 2, row % 2
    return p, h, c, x, (x + 2 * h) % 4


def device(p, h, c, u):
    return ((p + MERGES) % MERGES, 2 * h + c, (u + 2 * h) % 4)


def split(v):
    hi = v.astype(BF16)
    return hi, (v - hi.astype(F32)).astype(BF16)


def dot3(ah, al, bh, bl):
    d = lambda a, b: jnp.dot(a, b, preferred_element_type=F32)
    return d(ah, bh) + (d(ah, bl) + d(al, bh))


def pack(ref, v):
    ref[0:320] = v[:, 0:128]
    ref[320:640] = v[:, 128:256]
    ref[640:800] = jnp.concatenate([v[0:160, 256:320], v[160:320, 256:320]], axis=1)


def oblong(v):
    e = v[640:800]
    return jnp.concatenate([v[0:320], v[320:640], jnp.concatenate([e[:, 0:64], e[:, 64:128]], axis=0)], axis=1)


def flipped(v):
    return oblong(v).T


def ranks():
    return lax.broadcasted_iota(jnp.int32, (BLK, BLK), 0), lax.broadcasted_iota(jnp.int32, (BLK, BLK), 1)


def fold(ref, k):
    i, j = ranks()
    second = k[128:256, 128:256]
    ref[0:128] = jnp.where(i >= j, k[0:128, 0:128], second)
    ref[128:320] = k[128:320, 0:128]
    ref[320:384] = k[256:320, 128:256]
    ref[384:448] = jnp.concatenate([k[256:320, 256:320], jnp.zeros((64, 64), F32)], axis=1)
    ref[448:456] = jnp.broadcast_to(jnp.sum(jnp.where(i == j, second, 0.0), axis=0, keepdims=True), (8, BLK))


def square(v):
    i, j = ranks()
    m, a, b, e, d = v[0:128], v[128:320], v[320:384], v[384:448, 0:64], v[448:449]
    mt = m.T
    d0 = jnp.where(i >= j, m, mt)
    d1 = jnp.where(i < j, m, jnp.where(i > j, mt, d))
    r0 = jnp.concatenate([d0, a.T], axis=1)
    r1 = jnp.concatenate([a[0:128], d1, b.T], axis=1)
    r2 = jnp.concatenate([a[128:192], b, e], axis=1)
    return jnp.concatenate([r0, r1, r2], axis=0)


def refine_kernel(
    band, assign, s_hbm, k_hbm, refined, deviation,
    sp, lp, gd, go, s, k, ko, zb, zn, zs, lh, ll, sh, sl, th, tl, wh, wl, gh, gl, yh, yl_, ch, cl, local, send, recv,
):
    p, h, c, x, u = place()
    home = u < 2
    guest = u >= 2
    plane0 = h == 0
    plane1 = h == 1
    high = x >= 2
    diag_home = home & (u == c)
    off_home = home & (u != c)
    relay = guest & (c == 1)
    landing = home & (c == 1)
    holds_diag = c == x % 2
    first_off = jnp.where(home, u, 3 - u) != c
    other = device(p, h, 1 - c, u)
    used = [0]

    def copy(src, dst, to, which=0, ways=1, came=None):
        i = used[0] + which
        used[0] += ways
        return pltpu.make_async_remote_copy(
            src_ref=src, dst_ref=dst, send_sem=send.at[i], recv_sem=recv.at[i if came is None else came],
            device_id=to, device_id_type=MESH,
        )

    def on(cond, *acts):
        @pl.when(cond)
        def _():
            for act in acts:
                act()

    def cut(ref, n, parts):
        return [ref.at[pl.ds(i * (n // parts), n // parts)] for i in range(parts)]

    def copies(src, dst, n, parts, to):
        return [copy(a, b, to) for a, b in zip(cut(src, n, parts), cut(dst, n, parts))]

    load_k = pltpu.make_async_copy(k_hbm, k, local.at[0])
    load_s = pltpu.make_async_copy(s_hbm, s, local.at[1])
    load_k.start()
    load_s.start()
    barrier = pltpu.get_barrier_semaphore()
    friends = [device(p, 1 - h, c, (u + 2) % 4)]
    for q in (p - 1, p + 1):
        friends += [device(q, h, b, v) for v in range(4) for b in range(2)]
    friends += [device(p, h, b, (u + v) % 4) for v in range(4) for b in (c, 1 - c) if v or b is not c]
    for d in friends:
        pl.semaphore_signal(barrier, inc=1, device_id=d, device_id_type=MESH)
    last = (p == MERGES - 1) & plane1
    zeroth = (p == 0) & plane1
    seam = last | zeroth | ((p == 0) & plane0) | ((p == MERGES - 1) & plane0)

    @pl.when(seam)
    def _():
        for b in range(2):
            for v in range(4):
                d = (MERGES - 1 - p, 2 * (1 - h) + b, v)
                pl.semaphore_signal(barrier, inc=1, device_id=d, device_id_type=MESH)

    own_s = 2 * c + u % 2
    far_s = 2 * c + 1 - u % 2
    first = jnp.where(home, 2 * c + u, 2 * c + 3 - u)
    second = jnp.where(home, 2 * c + 1 - u, 2 * c + u - 2)

    load_k.wait()

    @pl.when(diag_home)
    def _():
        fold(gd.at[2], k)

    @pl.when(off_home)
    def _():
        pack(ko, k)

    @pl.when(home & plane0)
    def _():
        pack(lp.at[first], k)

    load_s.wait()
    pack(sp.at[own_s], s)

    NZ, NR, NL = 3, 5, 5
    step = PART // NR
    twin = device(p, 1 - h, c, (u + 2) % 4)
    r0 = copies(ko.at[pl.ds(0, PART)], zb, PART, NR, device(p, h, c, 3))
    r1 = copies(ko.at[pl.ds(PART, PART)], zb, PART, NR, device(p, h, c, 2))
    zo = copies(zb, zb, PART, NR, twin)
    zd = copies(gd.at[2], gd.at[jnp.where(plane0, 0, 2)], DIAG, NZ, twin)
    at_r = used[0]
    fr = copies(gd.at[2], gd.at[0], DIAG, NZ, device(p + 1, h, c, u))
    at_l = used[0]
    fl = copies(gd.at[2], gd.at[1], DIAG, NZ, device(p - 1, h, c, u))
    yr = copies(ko, go.at[0], OFFD, NL, device(p + 1, h, c, u))
    yl = copies(ko, go.at[1], OFFD, NL, device(p - 1, h, c, u))
    gs0 = copies(gd.at[0], gd.at[0], DIAG, NZ, other)
    gs1 = copies(gd.at[1], gd.at[1], DIAG, NZ, other)
    part = 1 - x % 2
    begin = pl.multiple_of(part * PART, 8)
    base = jnp.where(high, 0, 2)
    at_n = used[0]
    nr = copies(zb, zn.at[0], PART, NR, device(p + 1, h, c, u))
    nl = copies(zb, zn.at[1], PART, NR, device(p - 1, h, c, u))
    seam_r = [copy(a, b, (MERGES - 1 - p, c, x), came=at_n + i) for i, (a, b) in enumerate(zip(cut(zb, PART, NR), cut(zn.at[0], PART, NR)))]
    seam_l = [copy(a, b, (MERGES - 1 - p, c, x), came=at_n + NR + i) for i, (a, b) in enumerate(zip(cut(zb, PART, NR), cut(zn.at[1], PART, NR)))]
    spread = [[] for _ in range(NR)]
    chosen_spread = [[] for _ in range(NR)]
    at_go = used[0]
    for i in range(2):
        for j in range(NR):
            at = used[0]
            rows, dst = pl.ds(j * step, step), go.at[0, pl.ds(begin + j * step, step)]
            to = (p, 2 * h + 1 - i, base + i)
            spread[j].append(copy(zb.at[rows], dst, to, part, 2))
            used[0] = at
            chosen_spread[j].append(copy(zs.at[i, rows], dst, to, part, 2))

    def landed(n, j):
        i = at_go + j * 2 + n + (x % 2) * (2 * NR)
        return pltpu.make_async_remote_copy(
            src_ref=zb.at[pl.ds(0, step)], dst_ref=go.at[0, pl.ds(n * PART + j * step, step)],
            send_sem=send.at[i], recv_sem=recv.at[i], device_id=other, device_id_type=MESH,
        )

    came = [[landed(n, j) for j in range(NR)] for n in range(2)]
    sr = [copy(a, b, (MERGES - 1 - p, c, x), came=at_r + i) for i, (a, b) in enumerate(zip(cut(gd.at[2], DIAG, NZ), cut(gd.at[0], DIAG, NZ)))]
    sw = [copy(a, b, (MERGES - 1 - p, c, x), came=at_l + i) for i, (a, b) in enumerate(zip(cut(gd.at[2], DIAG, NZ), cut(gd.at[1], DIAG, NZ)))]
    os0 = copies(go.at[0], go.at[0], OFFD, 2, other)
    sx = copy(sp.at[own_s], sp.at[own_s], device(p, h, c, u + 1 - 2 * (u % 2)))
    sc0 = copy(sp.at[own_s], sp.at[own_s], other)
    sc1 = copy(sp.at[far_s], sp.at[far_s], other)
    hh = copies(lp.at[first], lp.at[first], OFFD, NL, device(p, h, c, 1 - u))
    hg = copies(lp.at[first], lp.at[first], OFFD, NL, device(p, h, c, 3 - u))
    gg = copies(lp.at[first], lp.at[first], OFFD, NL, device(p, h, c, 5 - u))[:3]
    hf = copies(lp.at[second], lp.at[second], OFFD, NL, device(p, h, c, 3 - u))[3:]
    ca = copy(lp.at[first], lp.at[first], other)
    cb = copy(lp.at[second], lp.at[second], other)

    starts = lambda cs: [d.start for d in cs]
    arrives = lambda cs: [d.wait_recv for d in cs]
    leaves = lambda cs: [d.wait_send for d in cs]
    both = lambda a, b: [d for pair in zip(a, b) for d in pair]
    flat = lambda a: [d for b in a for d in b]

    pl.semaphore_wait(barrier, len(friends) + 8 * seam.astype(jnp.int32))

    on(off_home & (u == 0), *starts(both(r0, r1)))
    y = p % 4
    on(diag_home & plane1, *starts(both(fr, fl)))
    on(diag_home & last, *starts(sr))
    on(diag_home & zeroth, *starts(sw))
    on(diag_home, *starts(zd))
    on(off_home & plane1, *starts(both(yr, yl)))
    on(home & plane0, *starts(hg), ca.start)
    on(diag_home & plane0, *starts(hh))
    on(guest | diag_home, sx.start)
    sc0.start()

    late = plane0 & ((y == 0) | (y == 3))
    for j in range(NR):
        on(relay & (u == 3), r0[j].wait_recv)
        on(relay & (u == 2), r1[j].wait_recv)
        on(relay & ~late, zo[j].start)
        on(relay & last, seam_r[j].start)
        on(relay & zeroth, seam_l[j].start)

    def pick(row, a, b):
        return jnp.where(assign[(5 * c + row // 64) // 2, p] == 0, a, b)

    @pl.when(diag_home & plane1)
    def _():
        for d in fr + fl:
            d.wait_recv()
        a, b = square(gd[0]), square(gd[1])
        pack(lp.at[first], jnp.concatenate([pick(i, a[i:i + 64], b[i:i + 64]) for i in range(0, 320, 64)], axis=0))
        for d in both(hg, hh) + [ca]:
            d.start()

    @pl.when(off_home & plane1)
    def _():
        edges = ((0, 64, 128, 160), (160, 192, 256, 320))
        for j in range(NL):
            yr[j].wait_recv()
            yl[j].wait_recv()
            if j < 4:
                e = edges[j % 2]
                for lo, hi in zip(e, e[1:]):
                    at = pl.ds(320 * (j // 2) + lo, hi - lo)
                    lp[first, at] = pick(lo, go[0, at], go[1, at])
            else:
                for lo, hi in ((0, 32), (32, 64), (64, 96), (96, 128), (128, 160)):
                    at = pl.ds(640 + lo, hi - lo)
                    a, b = go[0, at], go[1, at]
                    lp[first, at] = jnp.concatenate(
                        [pick(lo, a[:, 0:64], b[:, 0:64]), pick(160 + lo, a[:, 64:128], b[:, 64:128])], axis=1
                    )
            hg[j].start()
            hh[j].start()
        ca.start()

    on(guest | off_home, sx.wait_recv, sc1.start)

    for j in range(NL):
        on(guest, hg[j].wait_recv)
        if j < len(gg):
            on(guest & (plane1 | ~first_off), gg[j].start)
    on(relay & late, *starts(zo))
    on(guest, ca.start)
    on(home & (plane1 | first_off), *arrives(hh[3:]), *starts(hf), *arrives(hh[:3]), cb.start)
    on(guest & plane0 & first_off, *arrives(gg + hf), cb.start)

    for j in range(NZ):
        on(guest & plane0 & holds_diag, zd[j].wait_recv)
        on(guest & plane0 & holds_diag & (p < MERGES - 1), fr[j].start)
        on(guest & plane0 & holds_diag & (p > 0), fl[j].start)
        on(guest & plane1 & holds_diag, zd[j].wait_recv, gs0[j].start)
    for j in range(NR):
        on(landing, zo[j].wait_recv)
        on(landing & plane1, *starts(spread[j]))
        on(landing & plane0 & (p < MERGES - 1), nr[j].start)
        on(landing & plane0 & (p > 0), nl[j].start)

    @pl.when(landing & plane0)
    def _():
        lanes = lax.broadcasted_iota(jnp.int32, (16, BLK), 1)
        for j in range(NR):
            nr[j].wait_recv()
            nl[j].wait_recv()
            for g in range(step // 16):
                row = begin + j * step + g * 16
                slab, t = row // TILE, row % TILE
                low = assign[(5 + t // 64) // 2, p]
                up = assign[(5 + (t + 160 * (slab // 2)) // 64) // 2, p]
                at = pl.ds(j * step + g * 16, 16)
                a, b = zn[0, at], zn[1, at]
                zs[0, at] = jnp.where(jnp.where(lanes < 64, low, up) == 0, a, b)
                zs[1, at] = jnp.where(assign[slab, p] == 0, a, b)
            for d in chosen_spread[j]:
                d.start()

    sc0.wait_recv()
    on(guest | diag_home, sc1.wait_recv)

    @pl.when(home)
    def _():
        pack(sp.at[1 + u], flipped(sp[2 - u]))

    hc = x // 2
    cols = lax.broadcasted_iota(jnp.int32, (1, HALF), 1) // BLK
    begins = jnp.zeros((1, HALF), jnp.int32)
    for j in range(5):
        begins = jnp.where(cols == j, band[5 * hc + j], begins)
    cols = cols + 5 * hc
    for r in range(2):
        whole = jnp.concatenate([oblong(sp[2 * r]), oblong(sp[2 * r + 1])], axis=1)
        for i in range(5):
            bi = 5 * h + (5 * r + i) // 2
            st = band[bi]
            keep = ((cols >= st) & (cols < st + BAND)) | ((bi >= begins) & (bi < begins + BAND))
            rows = pl.ds(TILE * r + 64 * i, 64)
            sh[rows], sl[rows] = split(jnp.where(keep, whole[64 * i:64 * i + 64], 0.0))

    def left():
        @pl.when(plane0)
        def _():
            @pl.when((u == 0) | (u == 3))
            def _():
                pack(lp.at[1], flipped(lp[2]))

            @pl.when((u == 1) | (u == 2))
            def _():
                pack(lp.at[2], flipped(lp[1]))

        for r in range(2):
            rows = pl.ds(TILE * r, TILE)
            lh[rows], ll[rows] = split(jnp.concatenate([oblong(lp[2 * r]), oblong(lp[2 * r + 1])], axis=1))

    def right(r, v):
        rows = pl.ds(TILE * r, TILE)
        gh[rows], gl[rows] = split(v)

    def store_deviation(v):
        eye = lax.broadcasted_iota(jnp.int32, (TILE, TILE), 0) == lax.broadcasted_iota(jnp.int32, (TILE, TILE), 1)
        deviation[...] = jnp.where(eye & (2 * h + c == x), 1.0, 0.0) - v

    own_rows = pl.ds(pl.multiple_of(TILE * c, 64), TILE)

    def values_times_right():
        @pl.loop(0, 5)
        def _(i):
            rows = pl.ds(pl.multiple_of(i * 128, 128), 128)
            yh[rows], yl_[rows] = split(dot3(sh[rows], sl[rows], gh[...], gl[...]))

    def left_times_that():
        for r in range(2):
            rows = pl.ds(TILE * r, TILE)
            v = dot3(lh[rows], ll[rows], yh[...], yl_[...])
            ch[rows], cl[rows] = split(v)

            @pl.when(c == r)
            def _():
                store_deviation(v)

        return dot3(lh[own_rows], ll[own_rows], ch[...], cl[...])

    @pl.when(guest & plane0)
    def _():
        ca.wait_recv()

        @pl.when(~first_off)
        def _():
            cb.wait_recv()

        left()

        @pl.loop(0, 5)
        def _(i):
            rows = pl.ds(pl.multiple_of(i * 128, 128), 128)
            th[rows], tl[rows] = split(dot3(lh[rows], ll[rows], sh[...], sl[...]))

        wh[0:320], wl[0:320] = th[own_rows], tl[own_rows]
        for i in range(2):
            rows = pl.ds(pl.multiple_of(TILE * c + 160 * i, 32), 160)
            at = pl.ds(320 + 160 * i, 160)
            wh[at], wl[at] = split(dot3(lh[rows], ll[rows], th[...], tl[...]))

    on(guest & plane0 & holds_diag, *[a for j in range(NZ) for a in (fr[j].wait_recv, gs0[j].start, fl[j].wait_recv, gs1[j].start)])
    for n in range(2):
        on(guest & ~holds_diag, *arrives(came[n]), os0[n].start)
    on(guest & ~holds_diag, *arrives(gs0))
    on(guest & ~holds_diag & plane0, *arrives(gs1))
    on(guest & holds_diag, *arrives(os0))

    def chosen(r, unpack, ref):
        a, b = unpack(ref[0]), unpack(ref[1])
        out = []
        for j in range(5):
            sel = assign[(5 * r + j) // 2, p] == 0
            out.append(jnp.where(sel, a[64 * j:64 * j + 64], b[64 * j:64 * j + 64]))
        return jnp.concatenate(out, axis=0)

    @pl.when(guest & plane0)
    def _():
        @pl.when(u == 2)
        def _():
            right(0, chosen(0, square, gd))
            right(1, oblong(go[0]))

        @pl.when(u == 3)
        def _():
            right(0, flipped(go[0]))
            right(1, chosen(1, square, gd))

        store_deviation(dot3(wh[0:320], wl[0:320], gh[...], gl[...]))
        refined[...] = 1.5 * k[...] - 0.5 * dot3(wh[320:640], wl[320:640], gh[...], gl[...])

    @pl.when(guest & plane1)
    def _():
        @pl.when(u == 2)
        def _():
            right(0, square(gd[0]))
            right(1, oblong(go[0]))

        @pl.when(u == 3)
        def _():
            right(0, flipped(go[0]))
            right(1, square(gd[0]))

        values_times_right()
        for d in gg + hf:
            d.wait_recv()
        cb.start()
        ca.wait_recv()
        cb.wait_recv()
        left()
        refined[...] = 1.5 * k[...] - 0.5 * left_times_that()

    @pl.when(home)
    def _():
        ca.wait_recv()

        @pl.when(plane1 | (u == c))
        def _():
            cb.wait_recv()

        left()
        for r in range(2):
            right(r, oblong(lp[2 * r + u]))
        values_times_right()
        refined[...] = 1.5 * oblong(lp[2 * c + u]) - 0.5 * left_times_that()

    sc0.wait_send()
    ca.wait_send()
    on(guest | diag_home, sx.wait_send)
    on(guest | off_home, sc1.wait_send)
    on(plane1 | first_off, cb.wait_send)
    on(home & (plane1 | ~first_off), *leaves(hh))
    on(home & (plane1 | first_off), *leaves(hf))
    on(home, *leaves(hg))
    on(guest & (plane1 | ~first_off), *leaves(gg))
    on(diag_home, *leaves(zd))
    on(diag_home & plane1, *leaves(fr + fl))
    on(diag_home & last, *leaves(sr))
    on(diag_home & zeroth, *leaves(sw))
    on(guest & plane0 & holds_diag & (p < MERGES - 1), *leaves(fr))
    on(guest & plane0 & holds_diag & (p > 0), *leaves(fl))
    on(off_home & plane1, *leaves(yr + yl))
    on(off_home & (u == 0), *leaves(r0 + r1))
    on(relay, *leaves(zo))
    on(relay & last, *leaves(seam_r))
    on(relay & zeroth, *leaves(seam_l))
    on(landing & plane1, *leaves(flat(spread)))
    on(landing & plane0, *leaves(flat(chosen_spread)))
    on(landing & plane0 & (p < MERGES - 1), *leaves(nr))
    on(landing & plane0 & (p > 0), *leaves(nl))
    on(guest & ~holds_diag, *leaves(os0))
    on(guest & holds_diag, *leaves(gs0))
    on(guest & holds_diag & plane0, *leaves(gs1))


def hand_over_kernel(a, b, a_out, b_out):
    a_out[...] = a[...]
    b_out[...] = b[...]


def on_device(intersection, children, band_start, assignment):
    s, k = intersection[0], children[0]
    vm = pl.BlockSpec(memory_space=pltpu.VMEM)
    sm = pl.BlockSpec(memory_space=pltpu.SMEM)
    hb = pl.BlockSpec(memory_space=pltpu.HBM)
    shape = jax.ShapeDtypeStruct((TILE, TILE), F32)
    vmem = lambda *d: pltpu.VMEM(d, F32)
    half = lambda n: pltpu.VMEM((HALF, n), BF16)
    refined, deviation = pl.pallas_call(
        refine_kernel,
        out_shape=(shape, shape),
        in_specs=[sm, sm, hb, hb],
        out_specs=(vm, vm),
        scratch_shapes=[
            vmem(4, OFFD, BLK), vmem(4, OFFD, BLK), vmem(3, DIAG, BLK), vmem(2, OFFD, BLK),
            vmem(TILE, TILE), vmem(TILE, TILE), vmem(OFFD, BLK), vmem(PART, BLK), vmem(2, PART, BLK), vmem(2, PART, BLK),
        ]
        + [half(HALF)] * 8
        + [half(TILE)] * 6
        + [
            pltpu.SemaphoreType.DMA((2,)),
            pltpu.SemaphoreType.DMA((160,)),
            pltpu.SemaphoreType.DMA((160,)),
        ],
        compiler_params=pltpu.CompilerParams(
            collective_id=0, has_side_effects=True, vmem_limit_bytes=62 << 20
        ),
        name="refine",
    )(band_start, assignment.T, s, k)
    refined, deviation = pl.pallas_call(
        hand_over_kernel,
        out_shape=(shape, shape),
        in_specs=[vm, vm],
        out_specs=(vm, vm),
        compiler_params=pltpu.CompilerParams(vmem_limit_bytes=62 << 20),
        name="hand_over",
    )(refined, deviation)
    return refined[None], deviation[None]


def solution(mesh):
    spec = P("pair", "row", "col")
    return jax.shard_map(
        on_device, mesh=mesh, in_specs=(spec, spec, P(), P()), out_specs=(spec, spec), check_vma=False
    )
```

```python
import jax
import jax.numpy as jnp
from jax import lax
from jax.experimental import pallas as pl
from jax.experimental.pallas import tpu as pltpu
from jax.sharding import PartitionSpec as P

BLK = 128
BAND = 8
TILE = 320
HALF = 640
DIAG = 456
OFFD = 800
PART = 400
MERGES = 32
MESH = pl.DeviceIdType.MESH
F32 = jnp.float32
BF16 = jnp.bfloat16


def place():
    p = lax.axis_index("pair")
    row = lax.axis_index("row")
    x = lax.axis_index("col")
    h, c = row // 2, row % 2
    return p, h, c, x, (x + 2 * h) % 4


def device(p, h, c, u):
    return ((p + MERGES) % MERGES, 2 * h + c, (u + 2 * h) % 4)


def split(v):
    hi = v.astype(BF16)
    return hi, (v - hi.astype(F32)).astype(BF16)


def dot3(ah, al, bh, bl):
    d = lambda a, b: jnp.dot(a, b, preferred_element_type=F32)
    return d(ah, bh) + (d(ah, bl) + d(al, bh))


def pack(ref, v):
    ref[0:320] = v[:, 0:128]
    ref[320:640] = v[:, 128:256]
    ref[640:800] = jnp.concatenate([v[0:160, 256:320], v[160:320, 256:320]], axis=1)


def oblong(v):
    e = v[640:800]
    return jnp.concatenate([v[0:320], v[320:640], jnp.concatenate([e[:, 0:64], e[:, 64:128]], axis=0)], axis=1)


def flipped(v):
    return oblong(v).T


def ranks():
    return lax.broadcasted_iota(jnp.int32, (BLK, BLK), 0), lax.broadcasted_iota(jnp.int32, (BLK, BLK), 1)


def fold(ref, k):
    i, j = ranks()
    second = k[128:256, 128:256]
    ref[0:128] = jnp.where(i >= j, k[0:128, 0:128], second)
    ref[128:320] = k[128:320, 0:128]
    ref[320:384] = k[256:320, 128:256]
    ref[384:448] = jnp.concatenate([k[256:320, 256:320], jnp.zeros((64, 64), F32)], axis=1)
    ref[448:456] = jnp.broadcast_to(jnp.sum(jnp.where(i == j, second, 0.0), axis=0, keepdims=True), (8, BLK))


def square(v):
    i, j = ranks()
    m, a, b, e, d = v[0:128], v[128:320], v[320:384], v[384:448, 0:64], v[448:449]
    mt = m.T
    d0 = jnp.where(i >= j, m, mt)
    d1 = jnp.where(i < j, m, jnp.where(i > j, mt, d))
    r0 = jnp.concatenate([d0, a.T], axis=1)
    r1 = jnp.concatenate([a[0:128], d1, b.T], axis=1)
    r2 = jnp.concatenate([a[128:192], b, e], axis=1)
    return jnp.concatenate([r0, r1, r2], axis=0)


def refine_kernel(
    band, assign, s_hbm, k_hbm, refined, deviation,
    sp, lp, gd, go, s, k, ko, zb, zn, zs, lh, ll, sh, sl, th, tl, wh, wl, gh, gl, yh, yl_, ch, cl, local, send, recv,
):
    p, h, c, x, u = place()
    home = u < 2
    guest = u >= 2
    plane0 = h == 0
    plane1 = h == 1
    high = x >= 2
    diag_home = home & (u == c)
    off_home = home & (u != c)
    relay = guest & (c == 1)
    landing = home & (c == 1)
    holds_diag = c == x % 2
    first_off = jnp.where(home, u, 3 - u) != c
    other = device(p, h, 1 - c, u)
    used = [0]

    def copy(src, dst, to, which=0, ways=1, came=None):
        i = used[0] + which
        used[0] += ways
        return pltpu.make_async_remote_copy(
            src_ref=src, dst_ref=dst, send_sem=send.at[i], recv_sem=recv.at[i if came is None else came],
            device_id=to, device_id_type=MESH,
        )

    def on(cond, *acts):
        @pl.when(cond)
        def _():
            for act in acts:
                act()

    def cut(ref, n, parts):
        return [ref.at[pl.ds(i * (n // parts), n // parts)] for i in range(parts)]

    def copies(src, dst, n, parts, to):
        return [copy(a, b, to) for a, b in zip(cut(src, n, parts), cut(dst, n, parts))]

    load_k = pltpu.make_async_copy(k_hbm, k, local.at[0])
    load_s = pltpu.make_async_copy(s_hbm, s, local.at[1])
    load_k.start()
    load_s.start()
    barrier = pltpu.get_barrier_semaphore()
    friends = [device(p, 1 - h, c, (u + 2) % 4)]
    for q in (p - 1, p + 1):
        friends += [device(q, h, b, v) for v in range(4) for b in range(2)]
    friends += [device(p, h, b, (u + v) % 4) for v in range(4) for b in (c, 1 - c) if v or b is not c]
    for d in friends:
        pl.semaphore_signal(barrier, inc=1, device_id=d, device_id_type=MESH)
    last = (p == MERGES - 1) & plane1
    zeroth = (p == 0) & plane1
    seam = last | zeroth | ((p == 0) & plane0) | ((p == MERGES - 1) & plane0)

    @pl.when(seam)
    def _():
        for b in range(2):
            for v in range(4):
                d = (MERGES - 1 - p, 2 * (1 - h) + b, v)
                pl.semaphore_signal(barrier, inc=1, device_id=d, device_id_type=MESH)

    own_s = 2 * c + u % 2
    far_s = 2 * c + 1 - u % 2
    first = jnp.where(home, 2 * c + u, 2 * c + 3 - u)
    second = jnp.where(home, 2 * c + 1 - u, 2 * c + u - 2)

    load_k.wait()

    @pl.when(diag_home)
    def _():
        fold(gd.at[2], k)

    @pl.when(off_home)
    def _():
        pack(ko, k)

    @pl.when(home & plane0)
    def _():
        pack(lp.at[first], k)

    load_s.wait()
    pack(sp.at[own_s], s)

    NZ, NR, NL = 3, 5, 5
    step = PART // NR
    twin = device(p, 1 - h, c, (u + 2) % 4)
    r0 = copies(ko.at[pl.ds(0, PART)], zb, PART, NR, device(p, h, c, 3))
    r1 = copies(ko.at[pl.ds(PART, PART)], zb, PART, NR, device(p, h, c, 2))
    zo = copies(zb, zb, PART, NR, twin)
    zd = copies(gd.at[2], gd.at[jnp.where(plane0, 0, 2)], DIAG, NZ, twin)
    at_r = used[0]
    fr = copies(gd.at[2], gd.at[0], DIAG, NZ, device(p + 1, h, c, u))
    at_l = used[0]
    fl = copies(gd.at[2], gd.at[1], DIAG, NZ, device(p - 1, h, c, u))
    yr = copies(ko, go.at[0], OFFD, NL, device(p + 1, h, c, u))
    yl = copies(ko, go.at[1], OFFD, NL, device(p - 1, h, c, u))
    gs0 = copies(gd.at[0], gd.at[0], DIAG, NZ, other)
    gs1 = copies(gd.at[1], gd.at[1], DIAG, NZ, other)
    part = 1 - x % 2
    begin = pl.multiple_of(part * PART, 8)
    base = jnp.where(high, 0, 2)
    at_n = used[0]
    nr = copies(zb, zn.at[0], PART, NR, device(p + 1, h, c, u))
    nl = copies(zb, zn.at[1], PART, NR, device(p - 1, h, c, u))
    seam_r = [copy(a, b, (MERGES - 1 - p, c, x), came=at_n + i) for i, (a, b) in enumerate(zip(cut(zb, PART, NR), cut(zn.at[0], PART, NR)))]
    seam_l = [copy(a, b, (MERGES - 1 - p, c, x), came=at_n + NR + i) for i, (a, b) in enumerate(zip(cut(zb, PART, NR), cut(zn.at[1], PART, NR)))]
    spread = [[] for _ in range(NR)]
    chosen_spread = [[] for _ in range(NR)]
    at_go = used[0]
    for i in range(2):
        for j in range(NR):
            at = used[0]
            rows, dst = pl.ds(j * step, step), go.at[0, pl.ds(begin + j * step, step)]
            to = (p, 2 * h + 1 - i, base + i)
            spread[j].append(copy(zb.at[rows], dst, to, part, 2))
            used[0] = at
            chosen_spread[j].append(copy(zs.at[i, rows], dst, to, part, 2))

    def landed(n, j):
        i = at_go + j * 2 + n + (x % 2) * (2 * NR)
        return pltpu.make_async_remote_copy(
            src_ref=zb.at[pl.ds(0, step)], dst_ref=go.at[0, pl.ds(n * PART + j * step, step)],
            send_sem=send.at[i], recv_sem=recv.at[i], device_id=other, device_id_type=MESH,
        )

    came = [[landed(n, j) for j in range(NR)] for n in range(2)]
    sr = [copy(a, b, (MERGES - 1 - p, c, x), came=at_r + i) for i, (a, b) in enumerate(zip(cut(gd.at[2], DIAG, NZ), cut(gd.at[0], DIAG, NZ)))]
    sw = [copy(a, b, (MERGES - 1 - p, c, x), came=at_l + i) for i, (a, b) in enumerate(zip(cut(gd.at[2], DIAG, NZ), cut(gd.at[1], DIAG, NZ)))]
    os0 = copies(go.at[0], go.at[0], OFFD, 2, other)
    sx = copy(sp.at[own_s], sp.at[own_s], device(p, h, c, u + 1 - 2 * (u % 2)))
    sc0 = copy(sp.at[own_s], sp.at[own_s], other)
    sc1 = copy(sp.at[far_s], sp.at[far_s], other)
    hh = copies(lp.at[first], lp.at[first], OFFD, NL, device(p, h, c, 1 - u))
    hg = copies(lp.at[first], lp.at[first], OFFD, NL, device(p, h, c, 3 - u))
    gg = copies(lp.at[first], lp.at[first], OFFD, NL, device(p, h, c, 5 - u))[:3]
    hf = copies(lp.at[second], lp.at[second], OFFD, NL, device(p, h, c, 3 - u))[3:]
    ca = copy(lp.at[first], lp.at[first], other)
    cb = copy(lp.at[second], lp.at[second], other)

    starts = lambda cs: [d.start for d in cs]
    arrives = lambda cs: [d.wait_recv for d in cs]
    leaves = lambda cs: [d.wait_send for d in cs]
    both = lambda a, b: [d for pair in zip(a, b) for d in pair]
    flat = lambda a: [d for b in a for d in b]

    pl.semaphore_wait(barrier, len(friends) + 8 * seam.astype(jnp.int32))

    on(off_home & (u == 0), *starts(both(r0, r1)))
    y = p % 4
    on(diag_home & plane1, *starts(both(fr, fl)))
    on(diag_home & last, *starts(sr))
    on(diag_home & zeroth, *starts(sw))
    on(diag_home, *starts(zd))
    on(off_home & plane1, *starts(both(yr, yl)))
    on(home & plane0, *starts(hg), ca.start)
    on(diag_home & plane0, *starts(hh))
    on(guest | diag_home, sx.start)
    sc0.start()

    late = plane0 & ((y == 0) | (y == 3))
    for j in range(NR):
        on(relay & (u == 3), r0[j].wait_recv)
        on(relay & (u == 2), r1[j].wait_recv)
        on(relay & ~late, zo[j].start)
        on(relay & last, seam_r[j].start)
        on(relay & zeroth, seam_l[j].start)

    def pick(row, a, b):
        return jnp.where(assign[(5 * c + row // 64) // 2, p] == 0, a, b)

    @pl.when(diag_home & plane1)
    def _():
        for d in fr + fl:
            d.wait_recv()
        a, b = square(gd[0]), square(gd[1])
        pack(lp.at[first], jnp.concatenate([pick(i, a[i:i + 64], b[i:i + 64]) for i in range(0, 320, 64)], axis=0))
        for d in both(hg, hh) + [ca]:
            d.start()

    @pl.when(off_home & plane1)
    def _():
        edges = ((0, 64, 128, 160), (160, 192, 256, 320))
        for j in range(NL):
            yr[j].wait_recv()
            yl[j].wait_recv()
            if j < 4:
                e = edges[j % 2]
                for lo, hi in zip(e, e[1:]):
                    at = pl.ds(320 * (j // 2) + lo, hi - lo)
                    lp[first, at] = pick(lo, go[0, at], go[1, at])
            else:
                for lo, hi in ((0, 32), (32, 64), (64, 96), (96, 128), (128, 160)):
                    at = pl.ds(640 + lo, hi - lo)
                    a, b = go[0, at], go[1, at]
                    lp[first, at] = jnp.concatenate(
                        [pick(lo, a[:, 0:64], b[:, 0:64]), pick(160 + lo, a[:, 64:128], b[:, 64:128])], axis=1
                    )
            hg[j].start()
            hh[j].start()
        ca.start()

    on(guest | off_home, sx.wait_recv, sc1.start)

    for j in range(NL):
        on(guest, hg[j].wait_recv)
        on(relay & late, zo[j].start)
        if j < len(gg):
            on(guest & (plane1 | ~first_off), gg[j].start)
    on(guest, ca.start)
    on(home & (plane1 | first_off), *arrives(hh[3:]), *starts(hf), *arrives(hh[:3]), cb.start)
    on(guest & plane0 & first_off, *arrives(gg + hf), cb.start)

    for j in range(NZ):
        on(guest & plane0 & holds_diag, zd[j].wait_recv)
        on(guest & plane0 & holds_diag & (p < MERGES - 1), fr[j].start)
        on(guest & plane0 & holds_diag & (p > 0), fl[j].start)
        on(guest & plane1 & holds_diag, zd[j].wait_recv, gs0[j].start)
    for j in range(NR):
        on(landing, zo[j].wait_recv)
        on(landing & plane1, *starts(spread[j]))
        on(landing & plane0 & (p < MERGES - 1), nr[j].start)
        on(landing & plane0 & (p > 0), nl[j].start)

    @pl.when(landing & plane0)
    def _():
        lanes = lax.broadcasted_iota(jnp.int32, (16, BLK), 1)
        for j in range(NR):
            nr[j].wait_recv()
            nl[j].wait_recv()
            for g in range(step // 16):
                row = begin + j * step + g * 16
                slab, t = row // TILE, row % TILE
                low = assign[(5 + t // 64) // 2, p]
                up = assign[(5 + (t + 160 * (slab // 2)) // 64) // 2, p]
                at = pl.ds(j * step + g * 16, 16)
                a, b = zn[0, at], zn[1, at]
                zs[0, at] = jnp.where(jnp.where(lanes < 64, low, up) == 0, a, b)
                zs[1, at] = jnp.where(assign[slab, p] == 0, a, b)
            for d in chosen_spread[j]:
                d.start()

    sc0.wait_recv()
    on(guest | diag_home, sc1.wait_recv)

    @pl.when(home)
    def _():
        pack(sp.at[1 + u], flipped(sp[2 - u]))

    hc = x // 2
    cols = lax.broadcasted_iota(jnp.int32, (1, HALF), 1) // BLK
    begins = jnp.zeros((1, HALF), jnp.int32)
    for j in range(5):
        begins = jnp.where(cols == j, band[5 * hc + j], begins)
    cols = cols + 5 * hc
    for r in range(2):
        whole = jnp.concatenate([oblong(sp[2 * r]), oblong(sp[2 * r + 1])], axis=1)
        for i in range(5):
            bi = 5 * h + (5 * r + i) // 2
            st = band[bi]
            keep = ((cols >= st) & (cols < st + BAND)) | ((bi >= begins) & (bi < begins + BAND))
            rows = pl.ds(TILE * r + 64 * i, 64)
            sh[rows], sl[rows] = split(jnp.where(keep, whole[64 * i:64 * i + 64], 0.0))

    def left():
        @pl.when(plane0)
        def _():
            @pl.when((u == 0) | (u == 3))
            def _():
                pack(lp.at[1], flipped(lp[2]))

            @pl.when((u == 1) | (u == 2))
            def _():
                pack(lp.at[2], flipped(lp[1]))

        for r in range(2):
            rows = pl.ds(TILE * r, TILE)
            lh[rows], ll[rows] = split(jnp.concatenate([oblong(lp[2 * r]), oblong(lp[2 * r + 1])], axis=1))

    def right(r, v):
        rows = pl.ds(TILE * r, TILE)
        gh[rows], gl[rows] = split(v)

    def store_deviation(v):
        eye = lax.broadcasted_iota(jnp.int32, (TILE, TILE), 0) == lax.broadcasted_iota(jnp.int32, (TILE, TILE), 1)
        deviation[...] = jnp.where(eye & (2 * h + c == x), 1.0, 0.0) - v

    own_rows = pl.ds(pl.multiple_of(TILE * c, 64), TILE)

    def values_times_right():
        @pl.loop(0, 5)
        def _(i):
            rows = pl.ds(pl.multiple_of(i * 128, 128), 128)
            yh[rows], yl_[rows] = split(dot3(sh[rows], sl[rows], gh[...], gl[...]))

    def left_times_that():
        for r in range(2):
            rows = pl.ds(TILE * r, TILE)
            v = dot3(lh[rows], ll[rows], yh[...], yl_[...])
            ch[rows], cl[rows] = split(v)

            @pl.when(c == r)
            def _():
                store_deviation(v)

        return dot3(lh[own_rows], ll[own_rows], ch[...], cl[...])

    @pl.when(guest & plane0)
    def _():
        ca.wait_recv()

        @pl.when(~first_off)
        def _():
            cb.wait_recv()

        left()

        @pl.loop(0, 5)
        def _(i):
            rows = pl.ds(pl.multiple_of(i * 128, 128), 128)
            th[rows], tl[rows] = split(dot3(lh[rows], ll[rows], sh[...], sl[...]))

    on(guest & plane0 & holds_diag, *[a for j in range(NZ) for a in (fr[j].wait_recv, gs0[j].start, fl[j].wait_recv, gs1[j].start)])
    for n in range(2):
        on(guest & ~holds_diag, *arrives(came[n]), os0[n].start)

    @pl.when(guest & plane0)
    def _():
        wh[0:320], wl[0:320] = th[own_rows], tl[own_rows]
        for i in range(2):
            rows = pl.ds(pl.multiple_of(TILE * c + 160 * i, 32), 160)
            at = pl.ds(320 + 160 * i, 160)
            wh[at], wl[at] = split(dot3(lh[rows], ll[rows], th[...], tl[...]))

    on(guest & ~holds_diag, *arrives(gs0))
    on(guest & ~holds_diag & plane0, *arrives(gs1))
    on(guest & holds_diag, *arrives(os0))

    def chosen(r, unpack, ref):
        a, b = unpack(ref[0]), unpack(ref[1])
        out = []
        for j in range(5):
            sel = assign[(5 * r + j) // 2, p] == 0
            out.append(jnp.where(sel, a[64 * j:64 * j + 64], b[64 * j:64 * j + 64]))
        return jnp.concatenate(out, axis=0)

    @pl.when(guest & plane0)
    def _():
        @pl.when(u == 2)
        def _():
            right(0, chosen(0, square, gd))
            right(1, oblong(go[0]))

        @pl.when(u == 3)
        def _():
            right(0, flipped(go[0]))
            right(1, chosen(1, square, gd))

        store_deviation(dot3(wh[0:320], wl[0:320], gh[...], gl[...]))
        refined[...] = 1.5 * k[...] - 0.5 * dot3(wh[320:640], wl[320:640], gh[...], gl[...])

    @pl.when(guest & plane1)
    def _():
        @pl.when(u == 2)
        def _():
            right(0, square(gd[0]))
            right(1, oblong(go[0]))

        @pl.when(u == 3)
        def _():
            right(0, flipped(go[0]))
            right(1, square(gd[0]))

        values_times_right()
        for d in gg + hf:
            d.wait_recv()
        cb.start()
        ca.wait_recv()
        cb.wait_recv()
        left()
        refined[...] = 1.5 * k[...] - 0.5 * left_times_that()

    @pl.when(home)
    def _():
        ca.wait_recv()

        @pl.when(plane1 | (u == c))
        def _():
            cb.wait_recv()

        left()
        for r in range(2):
            right(r, oblong(lp[2 * r + u]))
        values_times_right()
        refined[...] = 1.5 * oblong(lp[2 * c + u]) - 0.5 * left_times_that()

    sc0.wait_send()
    ca.wait_send()
    on(guest | diag_home, sx.wait_send)
    on(guest | off_home, sc1.wait_send)
    on(plane1 | first_off, cb.wait_send)
    on(home & (plane1 | ~first_off), *leaves(hh))
    on(home & (plane1 | first_off), *leaves(hf))
    on(home, *leaves(hg))
    on(guest & (plane1 | ~first_off), *leaves(gg))
    on(diag_home, *leaves(zd))
    on(diag_home & plane1, *leaves(fr + fl))
    on(diag_home & last, *leaves(sr))
    on(diag_home & zeroth, *leaves(sw))
    on(guest & plane0 & holds_diag & (p < MERGES - 1), *leaves(fr))
    on(guest & plane0 & holds_diag & (p > 0), *leaves(fl))
    on(off_home & plane1, *leaves(yr + yl))
    on(off_home & (u == 0), *leaves(r0 + r1))
    on(relay, *leaves(zo))
    on(relay & last, *leaves(seam_r))
    on(relay & zeroth, *leaves(seam_l))
    on(landing & plane1, *leaves(flat(spread)))
    on(landing & plane0, *leaves(flat(chosen_spread)))
    on(landing & plane0 & (p < MERGES - 1), *leaves(nr))
    on(landing & plane0 & (p > 0), *leaves(nl))
    on(guest & ~holds_diag, *leaves(os0))
    on(guest & holds_diag, *leaves(gs0))
    on(guest & holds_diag & plane0, *leaves(gs1))


def hand_over_kernel(a, b, a_out, b_out):
    a_out[...] = a[...]
    b_out[...] = b[...]


def on_device(intersection, children, band_start, assignment):
    s, k = intersection[0], children[0]
    vm = pl.BlockSpec(memory_space=pltpu.VMEM)
    sm = pl.BlockSpec(memory_space=pltpu.SMEM)
    hb = pl.BlockSpec(memory_space=pltpu.HBM)
    shape = jax.ShapeDtypeStruct((TILE, TILE), F32)
    vmem = lambda *d: pltpu.VMEM(d, F32)
    half = lambda n: pltpu.VMEM((HALF, n), BF16)
    refined, deviation = pl.pallas_call(
        refine_kernel,
        out_shape=(shape, shape),
        in_specs=[sm, sm, hb, hb],
        out_specs=(vm, vm),
        scratch_shapes=[
            vmem(4, OFFD, BLK), vmem(4, OFFD, BLK), vmem(3, DIAG, BLK), vmem(2, OFFD, BLK),
            vmem(TILE, TILE), vmem(TILE, TILE), vmem(OFFD, BLK), vmem(PART, BLK), vmem(2, PART, BLK), vmem(2, PART, BLK),
        ]
        + [half(HALF)] * 8
        + [half(TILE)] * 6
        + [
            pltpu.SemaphoreType.DMA((2,)),
            pltpu.SemaphoreType.DMA((160,)),
            pltpu.SemaphoreType.DMA((160,)),
        ],
        compiler_params=pltpu.CompilerParams(
            collective_id=0, has_side_effects=True, vmem_limit_bytes=62 << 20
        ),
        name="refine",
    )(band_start, assignment.T, s, k)
    refined, deviation = pl.pallas_call(
        hand_over_kernel,
        out_shape=(shape, shape),
        in_specs=[vm, vm],
        out_specs=(vm, vm),
        compiler_params=pltpu.CompilerParams(vmem_limit_bytes=62 << 20),
        name="hand_over",
    )(refined, deviation)
    return refined[None], deviation[None]


def solution(mesh):
    spec = P("pair", "row", "col")
    return jax.shard_map(
        on_device, mesh=mesh, in_specs=(spec, spec, P(), P()), out_specs=(spec, spec), check_vma=False
    )
```

```python
import jax
import jax.numpy as jnp
from jax import lax
from jax.experimental import pallas as pl
from jax.experimental.pallas import tpu as pltpu
from jax.sharding import PartitionSpec as P

BLK = 128
BAND = 8
TILE = 320
HALF = 640
DIAG = 456
OFFD = 800
PART = 400
MERGES = 32
MESH = pl.DeviceIdType.MESH
F32 = jnp.float32
BF16 = jnp.bfloat16


def place():
    p = lax.axis_index("pair")
    row = lax.axis_index("row")
    x = lax.axis_index("col")
    h, c = row // 2, row % 2
    return p, h, c, x, (x + 2 * h) % 4


def device(p, h, c, u):
    return ((p + MERGES) % MERGES, 2 * h + c, (u + 2 * h) % 4)


def split(v):
    hi = v.astype(BF16)
    return hi, (v - hi.astype(F32)).astype(BF16)


def dot3(ah, al, bh, bl):
    n = ah.shape[0]
    d = lambda a, b: jnp.dot(a, b, preferred_element_type=F32)
    both = d(jnp.concatenate([ah, al], axis=0), bh)
    return both[:n] + (d(ah, bl) + both[n:])


def pack(ref, v):
    ref[0:320] = v[:, 0:128]
    ref[320:640] = v[:, 128:256]
    ref[640:800] = jnp.concatenate([v[0:160, 256:320], v[160:320, 256:320]], axis=1)


def oblong(v):
    e = v[640:800]
    return jnp.concatenate([v[0:320], v[320:640], jnp.concatenate([e[:, 0:64], e[:, 64:128]], axis=0)], axis=1)


def flipped(v):
    return oblong(v).T


def ranks():
    return lax.broadcasted_iota(jnp.int32, (BLK, BLK), 0), lax.broadcasted_iota(jnp.int32, (BLK, BLK), 1)


def fold(ref, k):
    i, j = ranks()
    second = k[128:256, 128:256]
    ref[0:128] = jnp.where(i >= j, k[0:128, 0:128], second)
    ref[128:320] = k[128:320, 0:128]
    ref[320:384] = k[256:320, 128:256]
    ref[384:448] = jnp.concatenate([k[256:320, 256:320], jnp.zeros((64, 64), F32)], axis=1)
    ref[448:456] = jnp.broadcast_to(jnp.sum(jnp.where(i == j, second, 0.0), axis=0, keepdims=True), (8, BLK))


def square(v):
    i, j = ranks()
    m, a, b, e, d = v[0:128], v[128:320], v[320:384], v[384:448, 0:64], v[448:449]
    mt = m.T
    d0 = jnp.where(i >= j, m, mt)
    d1 = jnp.where(i < j, m, jnp.where(i > j, mt, d))
    r0 = jnp.concatenate([d0, a.T], axis=1)
    r1 = jnp.concatenate([a[0:128], d1, b.T], axis=1)
    r2 = jnp.concatenate([a[128:192], b, e], axis=1)
    return jnp.concatenate([r0, r1, r2], axis=0)


def refine_kernel(
    band, assign, s_hbm, k_hbm, refined, deviation,
    sp, lp, gd, go, s, k, ko, zb, zn, zs, lh, ll, sh, sl, th, tl, wh, wl, gh, gl, yh, yl_, ch, cl, local, send, recv,
):
    p, h, c, x, u = place()
    home = u < 2
    guest = u >= 2
    plane0 = h == 0
    plane1 = h == 1
    high = x >= 2
    diag_home = home & (u == c)
    off_home = home & (u != c)
    relay = guest & (c == 1)
    landing = home & (c == 1)
    holds_diag = c == x % 2
    first_off = jnp.where(home, u, 3 - u) != c
    other = device(p, h, 1 - c, u)
    used = [0]

    def copy(src, dst, to, which=0, ways=1, came=None):
        i = used[0] + which
        used[0] += ways
        return pltpu.make_async_remote_copy(
            src_ref=src, dst_ref=dst, send_sem=send.at[i], recv_sem=recv.at[i if came is None else came],
            device_id=to, device_id_type=MESH,
        )

    def on(cond, *acts):
        @pl.when(cond)
        def _():
            for act in acts:
                act()

    def cut(ref, n, parts):
        return [ref.at[pl.ds(i * (n // parts), n // parts)] for i in range(parts)]

    def copies(src, dst, n, parts, to):
        return [copy(a, b, to) for a, b in zip(cut(src, n, parts), cut(dst, n, parts))]

    load_k = pltpu.make_async_copy(k_hbm, k, local.at[0])
    load_s = pltpu.make_async_copy(s_hbm, s, local.at[1])
    load_k.start()
    load_s.start()
    barrier = pltpu.get_barrier_semaphore()
    friends = [device(p, 1 - h, c, (u + 2) % 4)]
    for q in (p - 1, p + 1):
        friends += [device(q, h, b, v) for v in range(4) for b in range(2)]
    friends += [device(p, h, b, (u + v) % 4) for v in range(4) for b in (c, 1 - c) if v or b is not c]
    for d in friends:
        pl.semaphore_signal(barrier, inc=1, device_id=d, device_id_type=MESH)
    last = (p == MERGES - 1) & plane1
    zeroth = (p == 0) & plane1
    seam = last | zeroth | ((p == 0) & plane0) | ((p == MERGES - 1) & plane0)

    @pl.when(seam)
    def _():
        for b in range(2):
            for v in range(4):
                d = (MERGES - 1 - p, 2 * (1 - h) + b, v)
                pl.semaphore_signal(barrier, inc=1, device_id=d, device_id_type=MESH)

    own_s = 2 * c + u % 2
    far_s = 2 * c + 1 - u % 2
    first = jnp.where(home, 2 * c + u, 2 * c + 3 - u)
    second = jnp.where(home, 2 * c + 1 - u, 2 * c + u - 2)

    load_k.wait()

    @pl.when(diag_home)
    def _():
        fold(gd.at[2], k)

    @pl.when(off_home)
    def _():
        pack(ko, k)

    @pl.when(home & plane0)
    def _():
        pack(lp.at[first], k)

    load_s.wait()
    pack(sp.at[own_s], s)

    NZ, NR, NL = 3, 5, 5
    step = PART // NR
    twin = device(p, 1 - h, c, (u + 2) % 4)
    r0 = copies(ko.at[pl.ds(0, PART)], zb, PART, NR, device(p, h, c, 3))
    r1 = copies(ko.at[pl.ds(PART, PART)], zb, PART, NR, device(p, h, c, 2))
    zo = copies(zb, zb, PART, NR, twin)
    zd = copies(gd.at[2], gd.at[jnp.where(plane0, 0, 2)], DIAG, NZ, twin)
    at_r = used[0]
    fr = copies(gd.at[2], gd.at[0], DIAG, NZ, device(p + 1, h, c, u))
    at_l = used[0]
    fl = copies(gd.at[2], gd.at[1], DIAG, NZ, device(p - 1, h, c, u))
    yr = copies(ko, go.at[0], OFFD, NL, device(p + 1, h, c, u))
    yl = copies(ko, go.at[1], OFFD, NL, device(p - 1, h, c, u))
    gs0 = copies(gd.at[0], gd.at[0], DIAG, NZ, other)
    gs1 = copies(gd.at[1], gd.at[1], DIAG, NZ, other)
    part = 1 - x % 2
    begin = pl.multiple_of(part * PART, 8)
    base = jnp.where(high, 0, 2)
    at_n = used[0]
    nr = copies(zb, zn.at[0], PART, NR, device(p + 1, h, c, u))
    nl = copies(zb, zn.at[1], PART, NR, device(p - 1, h, c, u))
    seam_r = [copy(a, b, (MERGES - 1 - p, c, x), came=at_n + i) for i, (a, b) in enumerate(zip(cut(zb, PART, NR), cut(zn.at[0], PART, NR)))]
    seam_l = [copy(a, b, (MERGES - 1 - p, c, x), came=at_n + NR + i) for i, (a, b) in enumerate(zip(cut(zb, PART, NR), cut(zn.at[1], PART, NR)))]
    spread = [[] for _ in range(NR)]
    chosen_spread = [[] for _ in range(NR)]
    at_go = used[0]
    for i in range(2):
        for j in range(NR):
            at = used[0]
            rows, dst = pl.ds(j * step, step), go.at[0, pl.ds(begin + j * step, step)]
            to = (p, 2 * h + 1 - i, base + i)
            spread[j].append(copy(zb.at[rows], dst, to, part, 2))
            used[0] = at
            chosen_spread[j].append(copy(zs.at[i, rows], dst, to, part, 2))

    def landed(n, j):
        i = at_go + j * 2 + n + (x % 2) * (2 * NR)
        return pltpu.make_async_remote_copy(
            src_ref=zb.at[pl.ds(0, step)], dst_ref=go.at[0, pl.ds(n * PART + j * step, step)],
            send_sem=send.at[i], recv_sem=recv.at[i], device_id=other, device_id_type=MESH,
        )

    came = [[landed(n, j) for j in range(NR)] for n in range(2)]
    sr = [copy(a, b, (MERGES - 1 - p, c, x), came=at_r + i) for i, (a, b) in enumerate(zip(cut(gd.at[2], DIAG, NZ), cut(gd.at[0], DIAG, NZ)))]
    sw = [copy(a, b, (MERGES - 1 - p, c, x), came=at_l + i) for i, (a, b) in enumerate(zip(cut(gd.at[2], DIAG, NZ), cut(gd.at[1], DIAG, NZ)))]
    os0 = copies(go.at[0], go.at[0], OFFD, 2, other)
    sx = copy(sp.at[own_s], sp.at[own_s], device(p, h, c, u + 1 - 2 * (u % 2)))
    sc0 = copy(sp.at[own_s], sp.at[own_s], other)
    sc1 = copy(sp.at[far_s], sp.at[far_s], other)
    hh = copies(lp.at[first], lp.at[first], OFFD, NL, device(p, h, c, 1 - u))
    hg = copies(lp.at[first], lp.at[first], OFFD, NL, device(p, h, c, 3 - u))
    gg = copies(lp.at[first], lp.at[first], OFFD, NL, device(p, h, c, 5 - u))[:3]
    hf = copies(lp.at[second], lp.at[second], OFFD, NL, device(p, h, c, 3 - u))[3:]
    ca = copy(lp.at[first], lp.at[first], other)
    cb = copy(lp.at[second], lp.at[second], other)

    starts = lambda cs: [d.start for d in cs]
    arrives = lambda cs: [d.wait_recv for d in cs]
    leaves = lambda cs: [d.wait_send for d in cs]
    both = lambda a, b: [d for pair in zip(a, b) for d in pair]
    flat = lambda a: [d for b in a for d in b]

    pl.semaphore_wait(barrier, len(friends) + 8 * seam.astype(jnp.int32))

    on(diag_home & last, *starts(sr))
    on(diag_home & zeroth, *starts(sw))
    on(off_home & (u == 0), *starts(both(r0, r1)))
    y = p % 4
    on(diag_home & plane1, *starts(both(fr, fl)))
    on(diag_home, *starts(zd))
    on(off_home & plane1, *starts(both(yr, yl)))
    on(home & plane0, *starts(hg), ca.start)
    on(diag_home & plane0, *starts(hh))
    on(guest | diag_home, sx.start)
    sc0.start()

    late = plane0 & ((y == 0) | (y == 3))
    for j in range(NR):
        on(relay & (u == 3), r0[j].wait_recv)
        on(relay & (u == 2), r1[j].wait_recv)
        on(relay & last, seam_r[j].start)
        on(relay & zeroth, seam_l[j].start)
        on(relay & ~late, zo[j].start)

    def pick(row, a, b):
        return jnp.where(assign[(5 * c + row // 64) // 2, p] == 0, a, b)

    @pl.when(diag_home & plane1)
    def _():
        for d in fr + fl:
            d.wait_recv()
        a, b = square(gd[0]), square(gd[1])
        pack(lp.at[first], jnp.concatenate([pick(i, a[i:i + 64], b[i:i + 64]) for i in range(0, 320, 64)], axis=0))
        for d in both(hg, hh) + [ca]:
            d.start()

    @pl.when(off_home & plane1)
    def _():
        edges = ((0, 64, 128, 160), (160, 192, 256, 320))
        for j in range(NL):
            yr[j].wait_recv()
            yl[j].wait_recv()
            if j < 4:
                e = edges[j % 2]
                for lo, hi in zip(e, e[1:]):
                    at = pl.ds(320 * (j // 2) + lo, hi - lo)
                    lp[first, at] = pick(lo, go[0, at], go[1, at])
            else:
                for lo, hi in ((0, 32), (32, 64), (64, 96), (96, 128), (128, 160)):
                    at = pl.ds(640 + lo, hi - lo)
                    a, b = go[0, at], go[1, at]
                    lp[first, at] = jnp.concatenate(
                        [pick(lo, a[:, 0:64], b[:, 0:64]), pick(160 + lo, a[:, 64:128], b[:, 64:128])], axis=1
                    )
            hg[j].start()
            hh[j].start()
        ca.start()

    on(guest | off_home, sx.wait_recv, sc1.start)

    for j in range(NL):
        on(guest, hg[j].wait_recv)
        on(relay & late, zo[j].start)
        if j < len(gg):
            on(guest & (plane1 | ~first_off), gg[j].start)
    on(guest, ca.start)
    on(home & (plane1 | first_off), *arrives(hh[3:]), *starts(hf), *arrives(hh[:3]), cb.start)
    on(guest & plane0 & first_off, *arrives(gg + hf), cb.start)

    for j in range(NZ):
        on(guest & plane0 & holds_diag, zd[j].wait_recv)
        on(guest & plane0 & holds_diag & (p < MERGES - 1), fr[j].start)
        on(guest & plane0 & holds_diag & (p > 0), fl[j].start)
        on(guest & plane1 & holds_diag, zd[j].wait_recv, gs0[j].start)
    for j in range(NR):
        on(landing, zo[j].wait_recv)
        on(landing & plane1, *starts(spread[j]))
        on(landing & plane0 & (p < MERGES - 1), nr[j].start)
        on(landing & plane0 & (p > 0), nl[j].start)

    @pl.when(landing & plane0)
    def _():
        lanes = lax.broadcasted_iota(jnp.int32, (16, BLK), 1)
        for j in range(NR):
            nr[j].wait_recv()
            nl[j].wait_recv()
            for g in range(step // 16):
                row = begin + j * step + g * 16
                slab, t = row // TILE, row % TILE
                low = assign[(5 + t // 64) // 2, p]
                up = assign[(5 + (t + 160 * (slab // 2)) // 64) // 2, p]
                at = pl.ds(j * step + g * 16, 16)
                a, b = zn[0, at], zn[1, at]
                zs[0, at] = jnp.where(jnp.where(lanes < 64, low, up) == 0, a, b)
                zs[1, at] = jnp.where(assign[slab, p] == 0, a, b)
            for d in chosen_spread[j]:
                d.start()

    sc0.wait_recv()
    on(guest | diag_home, sc1.wait_recv)

    @pl.when(home)
    def _():
        pack(sp.at[1 + u], flipped(sp[2 - u]))

    hc = x // 2
    cols = lax.broadcasted_iota(jnp.int32, (1, HALF), 1) // BLK
    begins = jnp.zeros((1, HALF), jnp.int32)
    for j in range(5):
        begins = jnp.where(cols == j, band[5 * hc + j], begins)
    cols = cols + 5 * hc
    for r in range(2):
        whole = jnp.concatenate([oblong(sp[2 * r]), oblong(sp[2 * r + 1])], axis=1)
        for i in range(5):
            bi = 5 * h + (5 * r + i) // 2
            st = band[bi]
            keep = ((cols >= st) & (cols < st + BAND)) | ((bi >= begins) & (bi < begins + BAND))
            rows = pl.ds(TILE * r + 64 * i, 64)
            sh[rows], sl[rows] = split(jnp.where(keep, whole[64 * i:64 * i + 64], 0.0))

    def left():
        @pl.when(plane0)
        def _():
            @pl.when((u == 0) | (u == 3))
            def _():
                pack(lp.at[1], flipped(lp[2]))

            @pl.when((u == 1) | (u == 2))
            def _():
                pack(lp.at[2], flipped(lp[1]))

        for r in range(2):
            rows = pl.ds(TILE * r, TILE)
            lh[rows], ll[rows] = split(jnp.concatenate([oblong(lp[2 * r]), oblong(lp[2 * r + 1])], axis=1))

    def right(r, v):
        rows = pl.ds(TILE * r, TILE)
        gh[rows], gl[rows] = split(v)

    def store_deviation(v):
        eye = lax.broadcasted_iota(jnp.int32, (TILE, TILE), 0) == lax.broadcasted_iota(jnp.int32, (TILE, TILE), 1)
        deviation[...] = jnp.where(eye & (2 * h + c == x), 1.0, 0.0) - v

    own_rows = pl.ds(pl.multiple_of(TILE * c, 64), TILE)

    def values_times_right():
        @pl.loop(0, 5)
        def _(i):
            rows = pl.ds(pl.multiple_of(i * 128, 128), 128)
            yh[rows], yl_[rows] = split(dot3(sh[rows], sl[rows], gh[...], gl[...]))

    def left_times_that():
        for r in range(2):
            rows = pl.ds(TILE * r, TILE)
            v = dot3(lh[rows], ll[rows], yh[...], yl_[...])
            ch[rows], cl[rows] = split(v)

            @pl.when(c == r)
            def _():
                store_deviation(v)

        return dot3(lh[own_rows], ll[own_rows], ch[...], cl[...])

    @pl.when(guest & plane0)
    def _():
        ca.wait_recv()

        @pl.when(~first_off)
        def _():
            cb.wait_recv()

        left()

        @pl.loop(0, 5)
        def _(i):
            rows = pl.ds(pl.multiple_of(i * 128, 128), 128)
            th[rows], tl[rows] = split(dot3(lh[rows], ll[rows], sh[...], sl[...]))

    on(guest & plane0 & holds_diag, *[a for j in range(NZ) for a in (fr[j].wait_recv, gs0[j].start, fl[j].wait_recv, gs1[j].start)])
    for n in range(2):
        on(guest & ~holds_diag, *arrives(came[n]), os0[n].start)

    @pl.when(guest & plane0)
    def _():
        wh[0:320], wl[0:320] = th[own_rows], tl[own_rows]
        for i in range(2):
            rows = pl.ds(pl.multiple_of(TILE * c + 160 * i, 32), 160)
            at = pl.ds(320 + 160 * i, 160)
            wh[at], wl[at] = split(dot3(lh[rows], ll[rows], th[...], tl[...]))

    on(guest & ~holds_diag, *arrives(gs0))
    on(guest & ~holds_diag & plane0, *arrives(gs1))
    on(guest & holds_diag, *arrives(os0))

    def chosen(r, unpack, ref):
        a, b = unpack(ref[0]), unpack(ref[1])
        out = []
        for j in range(5):
            sel = assign[(5 * r + j) // 2, p] == 0
            out.append(jnp.where(sel, a[64 * j:64 * j + 64], b[64 * j:64 * j + 64]))
        return jnp.concatenate(out, axis=0)

    @pl.when(guest & plane0)
    def _():
        @pl.when(u == 2)
        def _():
            right(0, chosen(0, square, gd))
            right(1, oblong(go[0]))

        @pl.when(u == 3)
        def _():
            right(0, flipped(go[0]))
            right(1, chosen(1, square, gd))

        store_deviation(dot3(wh[0:320], wl[0:320], gh[...], gl[...]))
        refined[...] = 1.5 * k[...] - 0.5 * dot3(wh[320:640], wl[320:640], gh[...], gl[...])

    @pl.when(guest & plane1)
    def _():
        @pl.when(u == 2)
        def _():
            right(0, square(gd[0]))
            right(1, oblong(go[0]))

        @pl.when(u == 3)
        def _():
            right(0, flipped(go[0]))
            right(1, square(gd[0]))

        values_times_right()
        for d in gg + hf:
            d.wait_recv()
        cb.start()
        ca.wait_recv()
        cb.wait_recv()
        left()
        refined[...] = 1.5 * k[...] - 0.5 * left_times_that()

    @pl.when(home)
    def _():
        ca.wait_recv()

        @pl.when(plane1 | (u == c))
        def _():
            cb.wait_recv()

        left()
        for r in range(2):
            right(r, oblong(lp[2 * r + u]))
        values_times_right()
        refined[...] = 1.5 * oblong(lp[2 * c + u]) - 0.5 * left_times_that()

    sc0.wait_send()
    ca.wait_send()
    on(guest | diag_home, sx.wait_send)
    on(guest | off_home, sc1.wait_send)
    on(plane1 | first_off, cb.wait_send)
    on(home & (plane1 | ~first_off), *leaves(hh))
    on(home & (plane1 | first_off), *leaves(hf))
    on(home, *leaves(hg))
    on(guest & (plane1 | ~first_off), *leaves(gg))
    on(diag_home, *leaves(zd))
    on(diag_home & plane1, *leaves(fr + fl))
    on(diag_home & last, *leaves(sr))
    on(diag_home & zeroth, *leaves(sw))
    on(guest & plane0 & holds_diag & (p < MERGES - 1), *leaves(fr))
    on(guest & plane0 & holds_diag & (p > 0), *leaves(fl))
    on(off_home & plane1, *leaves(yr + yl))
    on(off_home & (u == 0), *leaves(r0 + r1))
    on(relay, *leaves(zo))
    on(relay & last, *leaves(seam_r))
    on(relay & zeroth, *leaves(seam_l))
    on(landing & plane1, *leaves(flat(spread)))
    on(landing & plane0, *leaves(flat(chosen_spread)))
    on(landing & plane0 & (p < MERGES - 1), *leaves(nr))
    on(landing & plane0 & (p > 0), *leaves(nl))
    on(guest & ~holds_diag, *leaves(os0))
    on(guest & holds_diag, *leaves(gs0))
    on(guest & holds_diag & plane0, *leaves(gs1))


def hand_over_kernel(a, b, a_out, b_out):
    a_out[...] = a[...]
    b_out[...] = b[...]


def on_device(intersection, children, band_start, assignment):
    s, k = intersection[0], children[0]
    vm = pl.BlockSpec(memory_space=pltpu.VMEM)
    sm = pl.BlockSpec(memory_space=pltpu.SMEM)
    hb = pl.BlockSpec(memory_space=pltpu.HBM)
    shape = jax.ShapeDtypeStruct((TILE, TILE), F32)
    vmem = lambda *d: pltpu.VMEM(d, F32)
    half = lambda n: pltpu.VMEM((HALF, n), BF16)
    refined, deviation = pl.pallas_call(
        refine_kernel,
        out_shape=(shape, shape),
        in_specs=[sm, sm, hb, hb],
        out_specs=(vm, vm),
        scratch_shapes=[
            vmem(4, OFFD, BLK), vmem(4, OFFD, BLK), vmem(3, DIAG, BLK), vmem(2, OFFD, BLK),
            vmem(TILE, TILE), vmem(TILE, TILE), vmem(OFFD, BLK), vmem(PART, BLK), vmem(2, PART, BLK), vmem(2, PART, BLK),
        ]
        + [half(HALF)] * 8
        + [half(TILE)] * 6
        + [
            pltpu.SemaphoreType.DMA((2,)),
            pltpu.SemaphoreType.DMA((160,)),
            pltpu.SemaphoreType.DMA((160,)),
        ],
        compiler_params=pltpu.CompilerParams(
            collective_id=0, has_side_effects=True, vmem_limit_bytes=62 << 20
        ),
        name="refine",
    )(band_start, assignment.T, s, k)
    refined, deviation = pl.pallas_call(
        hand_over_kernel,
        out_shape=(shape, shape),
        in_specs=[vm, vm],
        out_specs=(vm, vm),
        compiler_params=pltpu.CompilerParams(vmem_limit_bytes=62 << 20),
        name="hand_over",
    )(refined, deviation)
    return refined[None], deviation[None]


def solution(mesh):
    spec = P("pair", "row", "col")
    return jax.shard_map(
        on_device, mesh=mesh, in_specs=(spec, spec, P(), P()), out_specs=(spec, spec), check_vma=False
    )
```
